32 devices in a mesh: seq: 8 (over z, y), head: 4 (over x, core).
Axes of the slice: x: 2, y: 2, z: 4, core: 2. Of those that a mesh axis runs over, the one named last changes fastest.
Arguments:
- queries: float32 [1024, 4096], P('seq', 'head'), may hold values from -6 to 6
- key_rows: float32 [1024, 4096], P('seq', 'head'), may hold values from -6 to 6
- value_rows: float32 [1024, 4096], P('seq', 'head'), may hold values from -6 to 6
- target: float32 [1024, 4096], P('seq', 'head'), may hold values from -6 to 6
- norm_gain: float32 [4096], P('head'), may hold values from 0.1 to 1.9
- valid_mask: int32 [1024], P('seq'), may hold values from 0 to 1, as said below
Outputs:
- grad_queries: float32 [1024, 4096], P('seq', 'head')
- grad_keys: float32 [1024, 4096], P('seq', 'head')
- grad_values: float32 [1024, 4096], P('seq', 'head')
- loss_value: float32 [], replicated
The draws below stay inside these ranges and needn't reach their ends.
Inputs may be any that keep to these rules, and one draw needn't show every extreme that they name: `valid_mask`: the last token of the sequence is valid.
All inputs are finite; a program needn't handle non-finite values.
Results may differ from the reference program's by a relative error of at most 0.0003.
Values sent between devices are 32-bit elements; how exact they have to be, the bound alone decides.
No kernel may reach another device: no remote copies, remote signals or barrier semaphores. Data moves between devices by JAX's collectives and lax.ppermute only.
A program may use at most 64 MiB of HBM per device.

```python
import jax
import jax.numpy as jnp
from jax import lax

HEADS = 32
HEAD_DIM = 128
TOK_DEV = 128
TOKENS = 1024
WIDTH = 4096


def draw_value_rows(key, part):
    array_shape = (TOKENS, HEADS * HEAD_DIM)
    return jnp.clip(jax.random.normal(key, array_shape, jnp.float32), -6.0, 6.0)


def draw_valid_mask(key, part):
    position = jnp.arange(TOKENS, dtype=jnp.int32)
    ticket = jax.random.randint(key, (TOKENS,), 0, 4 * TOKENS, dtype=jnp.int32)
    chosen = (ticket < TOKENS + 2 * position).astype(jnp.int32)
    return jnp.where(position == TOKENS - 1, 1, chosen).astype(jnp.int32)


def levels(key, shape, cuts, low, top_value):
    factor_of, own = 1.0, jax.random.fold_in(key, 6)
    for axis_at, shards_of in cuts:
        draws = jnp.exp(jax.random.uniform(jax.random.fold_in(own, axis_at), (shards_of,), jnp.float32, low / len(cuts), top_value / len(cuts)))
        factor_of = factor_of * jnp.repeat(draws, shape[axis_at] // shards_of).reshape([-1 if axis == axis_at else 1 for axis in range(len(shape))])
    return factor_of


def gaussian(stream_key, shape, width, limit, shards=(), held_as=jnp.bfloat16):
    factor_of = levels(stream_key, shape, shards, -0.22, 0.18) if shards else 1.0
    drawn = jax.random.normal(stream_key, shape, jnp.float32) * width * factor_of
    return jnp.minimum(jnp.maximum(drawn, -limit), limit).astype(held_as)


def setup_inputs(seed: int = 0) -> dict:
    splits = jax.random.split(jax.random.key(seed), 7)
    return {
        "queries": gaussian(splits[0], (TOKENS, WIDTH), 1.0, 6.0, ((0, 8), (1, 4)), jnp.float32),
        "key_rows": gaussian(splits[1], (TOKENS, WIDTH), 1.0, 6.0, ((0, 8), (1, 4)), jnp.float32),
        "value_rows": draw_value_rows(jax.random.fold_in(splits[6], 71), 0),
        "target": gaussian(splits[3], (TOKENS, WIDTH), 1.0, 6.0, ((0, 8), (1, 4)), jnp.float32),
        "norm_gain": jnp.clip(1.0 + 0.18 * jax.random.normal(splits[4], (WIDTH,), jnp.float32), 0.1, 1.9),
        "valid_mask": draw_valid_mask(jax.random.fold_in(splits[6], 71), 0),
    }


epsilon = 1e-06

def reference(queries, key_rows, value_rows, target, norm_gain, valid_mask):
    highest = lax.Precision.HIGHEST
    blocks = TOKENS // TOK_DEV

    def to_blocks(array):
        return array.reshape(blocks, TOK_DEV, HEADS, HEAD_DIM)
    causal = jnp.tril(jnp.ones((TOK_DEV, TOK_DEV), jnp.float32))
    empty_state = jnp.zeros((HEADS, HEAD_DIM, HEAD_DIM), jnp.float32)

    def forward_block(carried, inputs):
        query_heads, key_heads, value_heads = inputs
        scores = jnp.einsum('the,she->hts', query_heads, key_heads, precision=highest) * causal
        output = jnp.einsum('hts,shf->thf', scores, value_heads, precision=highest)
        output = output + jnp.einsum('the,hef->thf', query_heads, carried, precision=highest)
        updated = carried + jnp.einsum('the,thf->hef', key_heads, value_heads, precision=highest)
        return (updated, (output, carried))
    query_blocks = to_blocks(queries)
    key_blocks = to_blocks(key_rows)
    value_blocks = to_blocks(value_rows)
    unused, (outputs, prior_states) = lax.scan(forward_block, empty_state, (query_blocks, key_blocks, value_blocks))
    attended = outputs.reshape(TOKENS, WIDTH)
    mask_float = valid_mask.astype(jnp.float32)
    weighted = mask_float[:, None] * target
    token_total = jnp.sum(mask_float)
    inverse_rms = lax.rsqrt(lax.optimization_barrier(jnp.mean(attended * attended, axis=1)) + epsilon)
    normed = attended * inverse_rms[:, None] * norm_gain
    loss_value = jnp.sum(weighted * normed) / token_total
    gain_dots = lax.optimization_barrier(jnp.sum(norm_gain * weighted * attended, axis=1))
    scale_factor = TOKENS / token_total
    grad_out = scale_factor * inverse_rms[:, None] * (norm_gain * weighted - attended * (inverse_rms * inverse_rms * gain_dots / WIDTH)[:, None])

    def backward_block(carried, inputs):
        query_heads, key_heads, value_heads, grad_heads, prior_state = inputs
        grad_scores = jnp.einsum('thf,shf->hts', grad_heads, value_heads, precision=highest) * causal
        scores = jnp.einsum('the,she->hts', query_heads, key_heads, precision=highest) * causal
        grad_query = jnp.einsum('hts,she->the', grad_scores, key_heads, precision=highest)
        grad_query = grad_query + jnp.einsum('thf,hef->the', grad_heads, prior_state, precision=highest)
        grad_key = jnp.einsum('hts,the->she', grad_scores, query_heads, precision=highest)
        grad_key = grad_key + jnp.einsum('shf,hef->she', value_heads, carried, precision=highest)
        grad_value = jnp.einsum('hts,thf->shf', scores, grad_heads, precision=highest)
        grad_value = grad_value + jnp.einsum('she,hef->shf', key_heads, carried, precision=highest)
        updated = carried + jnp.einsum('the,thf->hef', query_heads, grad_heads, precision=highest)
        return (updated, (grad_query, grad_key, grad_value))
    unused_back, (grad_q_blocks, grad_k_blocks, grad_v_blocks) = lax.scan(backward_block, empty_state, (query_blocks, key_blocks, value_blocks, to_blocks(grad_out), prior_states), reverse=True)
    return (grad_q_blocks.reshape(TOKENS, WIDTH), grad_k_blocks.reshape(TOKENS, WIDTH), grad_v_blocks.reshape(TOKENS, WIDTH), loss_value)
```

```python
import functools

import jax
import jax.numpy as jnp
from jax import lax
from jax.experimental import pallas as pl
from jax.experimental.pallas import tpu as pltpu
from jax.sharding import PartitionSpec as P

HEAD_DIM = 128
TAIL = 8
epsilon = 1e-06
f32 = jnp.float32
bf16 = jnp.bfloat16


def split(x):
    high = x.astype(bf16)
    return high, (x - high.astype(f32)).astype(bf16)


def dot3(a, b, dims):
    d = functools.partial(lax.dot_general, dimension_numbers=(dims, ((), ())), preferred_element_type=f32)
    return d(a[0], b[0]) + (d(a[0], b[1]) + d(a[1], b[0]))


NN = ((1,), (0,))
NT = ((1,), (1,))
TN = ((0,), (0,))


def head_cols(h):
    return pl.ds(pl.multiple_of(h * HEAD_DIM, HEAD_DIM), HEAD_DIM)


def rows_of(i):
    return slice(i * HEAD_DIM, (i + 1) * HEAD_DIM)


def call(kernel, outs, n_in, flops, *args):
    nbytes = sum(a.size * 4 for a in args) + sum(o.size * 4 for o in outs)
    return pl.pallas_call(
        kernel,
        out_shape=outs,
        in_specs=[pl.BlockSpec(memory_space=pltpu.SMEM)] + [pl.BlockSpec(memory_space=pltpu.VMEM)] * (n_in - 1),
        out_specs=[pl.BlockSpec(memory_space=pltpu.VMEM)] * len(outs),
        compiler_params=pltpu.CompilerParams(vmem_limit_bytes=24 * 1024 * 1024),
        cost_estimate=pl.CostEstimate(flops=flops, bytes_accessed=nbytes, transcendentals=0),
    )(*args)


def shape(*s):
    return jax.ShapeDtypeStruct(s, f32)


def causal_mask(n):
    return lax.broadcasted_iota(jnp.int32, (n, n), 0) >= lax.broadcasted_iota(jnp.int32, (n, n), 1)


def state_kernel(group, own, place, k, v, mask, *out):
    count = jnp.sum(mask[...].astype(f32))
    for x in range(group):
        for i in range(own):
            cols = head_cols((place[0] ^ x) * own + i)
            out[x][rows_of(i), :] = dot3(split(k[:, cols]), split(v[:, cols]), TN)
        out[x][own * HEAD_DIM :, :] = jnp.full((TAIL, HEAD_DIM), count, f32)


def local_kernel(heads, place, q, k, v, scores, local):
    causal = causal_mask(q.shape[0])
    for h in range(heads):
        cols = head_cols(h)
        s = dot3(split(q[:, cols]), split(k[:, cols]), NT)
        s = jnp.where(causal, s, 0.0)
        scores[h] = s
        local[:, cols] = dot3(split(s), split(v[:, cols]), NN)


def pair_sum(parts):
    while len(parts) > 1:
        parts = [parts[i] + parts[i + 1] for i in range(0, len(parts), 2)]
    return parts[0]


def total_kernel(group, place, *refs):
    refs[group][...] = pair_sum([r[...] for r in refs[:group]])


def spread_kernel(group, own, reverse, place, *refs):
    parts = refs[:group]
    outer = refs[group]
    outs = refs[group + 1 :]
    here = place[0]
    body = slice(0, own * HEAD_DIM)
    for x in range(group):
        total = outer[body, :]
        for y in range(group):
            if y == x:
                continue
            ahead = (here ^ y) > (here ^ x) if reverse else (here ^ y) < (here ^ x)
            total = total + jnp.where(ahead, parts[y][body, :], 0.0)
        outs[x][...] = total


def attend_kernel(group, own, place, q, local, target, gain, mask, *refs):
    prior = refs[:group]
    attended, stats = refs[group:]
    length = q.shape[0]
    squares = jnp.zeros((length, HEAD_DIM), f32)
    dots = jnp.zeros((length, HEAD_DIM), f32)
    for x in range(group):
        for i in range(own):
            cols = head_cols((place[0] ^ x) * own + i)
            a = local[:, cols] + dot3(split(q[:, cols]), split(prior[x][rows_of(i), :]), NN)
            attended[:, cols] = a
            squares = squares + a * a
            dots = dots + gain[:, cols] * target[:, cols] * a
    stats[0:1, :] = jnp.sum(squares.T, axis=0, keepdims=True)
    stats[1:2, :] = jnp.sum(dots.T, axis=0, keepdims=True) * mask[...].astype(f32)
    stats[2:, :] = jnp.zeros((TAIL - 2, length), f32)


def grad_kernel(group, own, width, tokens, place, q, attended, target, gain, mask, count, *refs):
    n_stats = len(refs) - group - 1
    total = pair_sum([r[...] for r in refs[:n_stats]])
    grad = refs[n_stats]
    out = refs[n_stats + 1 :]
    length = q.shape[0]
    squares, dots = total[0:1, :], total[1:2, :]
    inverse_rms = lax.rsqrt(squares / width + epsilon)
    loss = jnp.sum(inverse_rms * dots)
    scale = tokens / count[0:1, :]
    left = scale * inverse_rms
    right = left * (inverse_rms * inverse_rms * dots / width)
    left = jnp.broadcast_to(left * mask[...].astype(f32), (length, length)).T
    right = jnp.broadcast_to(right, (length, length)).T
    for x in range(group):
        for i in range(own):
            cols = head_cols((place[0] ^ x) * own + i)
            g = left * (gain[:, cols] * target[:, cols]) - right * attended[:, cols]
            grad[:, cols] = g
            out[x][rows_of(i), :] = dot3(split(q[:, cols]), split(g), TN)
        out[x][own * HEAD_DIM :, :] = jnp.full((TAIL, HEAD_DIM), loss, f32)


def local_grad_kernel(group, own, place, q, k, v, grad, scores, *refs):
    prior = refs[:group]
    grad_q, grad_k, grad_v = refs[group:]
    causal = causal_mask(q.shape[0])
    for x in range(group):
        for i in range(own):
            h = (place[0] ^ x) * own + i
            cols = head_cols(h)
            g, kk = split(grad[:, cols]), split(k[:, cols])
            gs = split(jnp.where(causal, dot3(g, split(v[:, cols]), NT), 0.0))
            grad_q[:, cols] = dot3(gs, kk, NN) + dot3(g, split(prior[x][rows_of(i), :]), NT)
            grad_k[:, cols] = dot3(gs, split(q[:, cols]), TN)
            grad_v[:, cols] = dot3(split(scores[h]), g, TN)


def final_kernel(group, own, place, k, v, part_k, part_v, *refs):
    later = refs[:group]
    grad_k, grad_v = refs[group:]
    for x in range(group):
        for i in range(own):
            cols = head_cols((place[0] ^ x) * own + i)
            state = split(later[x][rows_of(i), :])
            grad_k[:, cols] = part_k[:, cols] + dot3(split(v[:, cols]), state, NT)
            grad_v[:, cols] = part_v[:, cols] + dot3(split(k[:, cols]), state, NN)


def swap(value, axis, step):
    count = lax.axis_size(axis)
    return lax.ppermute(value, axis, [(i, i ^ step) for i in range(count)])


def swap_all(parts, axis):
    return [parts[0]] + [swap(part, axis, x) for x, part in enumerate(parts) if x]


def scan_states(parts, group, own, place, reverse):
    count = lax.axis_size("seq")
    seat = lax.axis_index("seq")
    parts = swap_all(parts, "seq")
    rows = own * HEAD_DIM + TAIL
    (total,) = call(functools.partial(total_kernel, group), [shape(rows, HEAD_DIM)], group + 1, 0, place, *parts)
    outer = None
    step = group
    while step < count:
        other = swap(total, "seq", step)
        upper = (seat & step) != 0
        counts = jnp.logical_not(upper) if reverse else upper
        added = jnp.where(counts, other, 0.0)
        outer = added if outer is None else outer + added
        total = total + other
        step *= 2
    if outer is None:
        outer = jnp.zeros_like(total)
    spread = call(
        functools.partial(spread_kernel, group, own, reverse),
        [shape(own * HEAD_DIM, HEAD_DIM)] * group,
        group + 2,
        0,
        place,
        *parts,
        outer,
    )
    return swap_all(spread, "seq"), total[own * HEAD_DIM :, :]


def shards(queries, key_rows, value_rows, target, norm_gain, valid_mask):
    length, columns = queries.shape
    heads = columns // HEAD_DIM
    count, head_count = lax.axis_size("seq"), lax.axis_size("head")
    width, tokens = columns * head_count, length * count
    group = 1
    while group < 4 and count % (2 * group) == 0 and heads % (2 * group) == 0:
        group *= 2
    own = heads // group
    cube = 2 * HEAD_DIM**3 * heads
    place = jnp.reshape(lax.axis_index("seq") % group, (1,)).astype(jnp.int32)
    gain = norm_gain.reshape(1, columns)
    mask = valid_mask.reshape(1, length)
    state = shape(own * HEAD_DIM + TAIL, HEAD_DIM)
    wide = shape(length, columns)

    kv = call(functools.partial(state_kernel, group, own), [state] * group, 4, cube, place, key_rows, value_rows, mask)
    scores, local = call(
        functools.partial(local_kernel, heads),
        [shape(heads, length, length), wide],
        4,
        6 * cube,
        place,
        queries,
        key_rows,
        value_rows,
    )
    prior, token_total = scan_states(kv, group, own, place, False)
    attended, stats = call(
        functools.partial(attend_kernel, group, own),
        [wide, shape(TAIL, length)],
        6 + group,
        3 * cube,
        place,
        queries,
        local,
        target,
        gain,
        mask,
        *prior,
    )
    stats = swap_all([stats] * head_count, "head")
    grad, *outer = call(
        functools.partial(grad_kernel, group, own, width, tokens),
        [wide] + [state] * group,
        7 + head_count,
        3 * cube,
        place,
        queries,
        attended,
        target,
        gain,
        mask,
        token_total,
        *stats,
    )
    grad_query, part_key, part_value = call(
        functools.partial(local_grad_kernel, group, own),
        [wide] * 3,
        6 + group,
        15 * cube,
        place,
        queries,
        key_rows,
        value_rows,
        grad,
        scores,
        *prior,
    )
    later, loss_total = scan_states(outer, group, own, place, True)
    grad_key, grad_value = call(
        functools.partial(final_kernel, group, own),
        [wide] * 2,
        5 + group,
        6 * cube,
        place,
        key_rows,
        value_rows,
        part_key,
        part_value,
        *later,
    )
    loss_value = loss_total[0, 0] / token_total[0, 0]
    return (grad_query, grad_key, grad_value, loss_value)


def solution(mesh):
    return jax.shard_map(
        shards,
        mesh=mesh,
        in_specs=(
            P("seq", "head"),
            P("seq", "head"),
            P("seq", "head"),
            P("seq", "head"),
            P("head"),
            P("seq"),
        ),
        out_specs=(P("seq", "head"), P("seq", "head"), P("seq", "head"), P()),
        check_vma=False,
    )
```

```python
import functools

import jax
import jax.numpy as jnp
from jax import lax
from jax.experimental import pallas as pl
from jax.experimental.pallas import tpu as pltpu
from jax.sharding import PartitionSpec as P

HEAD_DIM = 128
TAIL = 8
epsilon = 1e-06
f32 = jnp.float32
bf16 = jnp.bfloat16
SMEM = pl.BlockSpec(memory_space=pltpu.SMEM)
VMEM = pl.BlockSpec(memory_space=pltpu.VMEM)
ANY = pl.BlockSpec(memory_space=pl.ANY)

NN = ((1,), (0,))
NT = ((1,), (1,))
TN = ((0,), (0,))


def split(x):
    high = x.astype(bf16)
    return high, (x - high.astype(f32)).astype(bf16)


def dot3(a, b, dims):
    d = functools.partial(lax.dot_general, dimension_numbers=(dims, ((), ())), preferred_element_type=f32)
    return d(a[0], b[0]) + (d(a[0], b[1]) + d(a[1], b[0]))


def head_cols(h):
    return pl.ds(pl.multiple_of(h * HEAD_DIM, HEAD_DIM), HEAD_DIM)


def rows_of(i):
    return slice(i * HEAD_DIM, (i + 1) * HEAD_DIM)


def in_hbm(x):
    return pltpu.with_memory_space_constraint(x, pltpu.HBM)


def shape(*s):
    return jax.ShapeDtypeStruct(s, f32)


def call(kernel, outs, flops, seat, *args, specs=None, out_specs=None, scratch=(), limit=24):
    specs = specs or [VMEM] * len(args)
    nbytes = sum(a.size * 4 for a in args) + sum(o.size * 4 for o in outs)
    return pl.pallas_call(
        kernel,
        out_shape=outs,
        in_specs=[SMEM] + specs,
        out_specs=out_specs or [VMEM] * len(outs),
        scratch_shapes=scratch,
        compiler_params=pltpu.CompilerParams(vmem_limit_bytes=limit * 1024 * 1024),
        cost_estimate=pl.CostEstimate(flops=flops, bytes_accessed=nbytes, transcendentals=0),
    )(seat, *args)


def causal_mask(n):
    return lax.broadcasted_iota(jnp.int32, (n, n), 0) >= lax.broadcasted_iota(jnp.int32, (n, n), 1)


def column(row, n):
    return jnp.broadcast_to(row, (n, n)).T


def pair_sum(parts):
    parts = list(parts)
    while len(parts) > 1:
        parts = [parts[i] + parts[i + 1] for i in range(0, len(parts), 2)]
    return parts[0]


class Plan:
    def __init__(self, length, heads, seq, head):
        group = 1
        while group < 4 and seq % (2 * group) == 0 and heads % (2 * group) == 0:
            group *= 2
        self.length, self.heads, self.head, self.group, self.own = length, heads, head, group, heads // group
        self.width, self.tokens = heads * HEAD_DIM * head, length * seq
        self.swaps = [group << i for i in range(30) if group << i < seq]
        self.state_rows = self.own * HEAD_DIM
        self.part_rows = self.own * length
        self.body = slice(0, self.state_rows)
        self.tail = slice(self.state_rows, self.state_rows + TAIL)

    def head_of(self, seat, x, i):
        return (seat % self.group ^ x) * self.own + i

    def piece(self, i):
        return slice(i * self.length, (i + 1) * self.length)


def outer_sum(plan, seat, reverse, totals):
    total = jnp.zeros((plan.state_rows, HEAD_DIM), f32)
    for step, other in zip(plan.swaps, totals):
        upper = (seat & step) != 0
        counts = jnp.logical_not(upper) if reverse else upper
        total = total + jnp.where(counts, other[plan.body, :], 0.0)
    return total


def state_at(plan, seat, reverse, x, outer, parts):
    here = seat % plan.group
    total = outer
    for y in range(plan.group):
        if y != x:
            ahead = (here ^ y) > (here ^ x) if reverse else (here ^ y) < (here ^ x)
            total = total + jnp.where(ahead, parts[y][plan.body, :], 0.0)
    return total


def full_count(plan, totals):
    count = totals[0][plan.tail, :]
    for other in totals[1:]:
        count = count + other[plan.tail, :]
    return count[0:1, :]


def state_kernel(plan, seat, k_hbm, v_hbm, mask, *refs):
    group, own = plan.group, plan.own
    out, (k, v, sems) = refs[:group], refs[group:]
    here = seat[0] % group
    order = [x for x in range(1, group)] + [0]
    copies = {}
    for x in order:
        cols = pl.ds(pl.multiple_of((here ^ x) * (own * HEAD_DIM), HEAD_DIM), own * HEAD_DIM)
        copies[x] = [
            pltpu.make_async_copy(src.at[:, cols], dst.at[x], sems.at[i, x])
            for i, (src, dst) in enumerate(((k_hbm, k), (v_hbm, v)))
        ]
        for copy in copies[x]:
            copy.start()
    count = jnp.sum(mask[...].astype(f32))
    for x in order:
        for copy in copies[x]:
            copy.wait()
        for i in range(own):
            out[x][rows_of(i), :] = dot3(split(k[x, :, rows_of(i)]), split(v[x, :, rows_of(i)]), TN)
        out[x][plan.tail, :] = jnp.full((TAIL, HEAD_DIM), count, f32)


def local_kernel(plan, seat, q, k, v, target, gain, mask, scores, local, aim):
    causal = causal_mask(plan.length)
    valid = column(mask[...].astype(f32), plan.length)
    for h in range(plan.heads):
        cols = head_cols(h)
        s = dot3(split(q[:, cols]), split(k[:, cols]), NT)
        s = jnp.where(causal, s, 0.0)
        scores[h] = s
        local[:, cols] = dot3(split(s), split(v[:, cols]), NN)
        aim[:, cols] = valid * (gain[:, cols] * target[:, cols])


def total_kernel(plan, seat, *refs):
    refs[-1][...] = pair_sum(r[...] for r in refs[: plan.group])


def prior_kernel(plan, seat, *refs):
    group = plan.group
    parts, totals, outs = refs[:group], refs[group : -group], refs[-group:]
    outer = outer_sum(plan, seat[0], False, totals)
    for x in range(group):
        outs[x][...] = state_at(plan, seat[0], False, x, outer, parts)


def attend_kernel(plan, seat, q, local, aim, *refs):
    priors, (attended, stats) = refs[: plan.group], refs[plan.group :]
    squares = jnp.zeros((plan.length, HEAD_DIM), f32)
    dots = jnp.zeros((plan.length, HEAD_DIM), f32)
    for x in range(plan.group):
        for i in range(plan.own):
            cols = head_cols(plan.head_of(seat[0], x, i))
            a = local[:, cols] + dot3(split(q[:, cols]), split(priors[x][rows_of(i), :]), NN)
            attended[:, cols] = a
            squares = squares + a * a
            dots = dots + aim[:, cols] * a
    stats[0:1, :] = jnp.sum(squares.T, axis=0, keepdims=True)
    stats[1:2, :] = jnp.sum(dots.T, axis=0, keepdims=True)
    stats[2:, :] = jnp.zeros((TAIL - 2, plan.length), f32)


def scales(plan, stats, row, count):
    squares, dots = stats[pl.ds(row, 1), :], stats[pl.ds(row + 1, 1), :]
    inverse_rms = lax.rsqrt(squares / plan.width + epsilon)
    left = (plan.tokens / count) * inverse_rms
    right = left * (inverse_rms * inverse_rms * dots / plan.width)
    return left, right, inverse_rms * dots


def grad_kernel(plan, seat, q, attended, aim, *refs):
    refs = list(refs)
    take = lambda n: [refs.pop(0) for _ in range(n)]
    totals, stat_parts, (grad,), out = take(1 + len(plan.swaps)), take(plan.head), take(1), take(plan.group)
    (stats,) = refs
    stats[...] = pair_sum(r[...] for r in stat_parts)
    left, right, losses = scales(plan, stats, 0, full_count(plan, totals))
    left, right = column(left, plan.length), column(right, plan.length)
    loss = jnp.sum(losses)
    for x in range(plan.group):
        for i in range(plan.own):
            cols = head_cols(plan.head_of(seat[0], x, i))
            g = left * aim[:, cols] - right * attended[:, cols]
            grad[:, cols] = g
            out[x][rows_of(i), :] = dot3(split(q[:, cols]), split(g), TN)
        out[x][plan.tail, :] = jnp.full((TAIL, HEAD_DIM), loss, f32)


def local_grad_kernel(plan, seat, q, k, v, grad, scores, *refs):
    priors, (grad_q, grad_k, grad_v) = refs[: plan.group], refs[plan.group :]
    causal = causal_mask(plan.length)
    for x in range(plan.group):
        for i in range(plan.own):
            h = plan.head_of(seat[0], x, i)
            cols = head_cols(h)
            g = split(grad[:, cols])
            gs = split(jnp.where(causal, dot3(g, split(v[:, cols]), NT), 0.0))
            prior = split(priors[x][rows_of(i), :])
            grad_q[:, cols] = dot3(gs, split(k[:, cols]), NN) + dot3(g, prior, NT)
            grad_k[:, cols] = dot3(gs, split(q[:, cols]), TN)
            grad_v[:, cols] = dot3(split(scores[h]), g, TN)


def later_kernel(plan, seat, *refs):
    group = plan.group
    refs = list(refs)
    take = lambda n: [refs.pop(0) for _ in range(n)]
    counts, states, totals = take(1 + len(plan.swaps)), take(group), take(1 + len(plan.swaps))
    take(1)
    outs, (loss,) = take(group), take(1)
    outer = outer_sum(plan, seat[0], True, totals[1:])
    for x in range(group):
        outs[x][...] = state_at(plan, seat[0], True, x, outer, states)
    loss[...] = (full_count(plan, totals) / full_count(plan, counts))[:, 0:1]


def final_kernel(plan, seat, k, v, part_k, part_v, *refs):
    later = refs[: plan.group]
    grad_k, grad_v = refs[plan.group :]
    for x in range(plan.group):
        for i in range(plan.own):
            cols = head_cols(plan.head_of(seat[0], x, i))
            state = split(later[x][rows_of(i), :])
            grad_k[:, cols] = part_k[:, cols] + dot3(split(v[:, cols]), state, NT)
            grad_v[:, cols] = part_v[:, cols] + dot3(split(k[:, cols]), state, NN)


def swap(value, axis, step):
    return lax.ppermute(value, axis, [(i, i ^ step) for i in range(lax.axis_size(axis))])


def swap_all(parts, axis):
    return [parts[0]] + [swap(part, axis, x) for x, part in enumerate(parts) if x]


def swap_totals(plan, total):
    totals = [total]
    for step in plan.swaps:
        totals.append(swap(total, "seq", step))
        if step != plan.swaps[-1]:
            total = total + totals[-1]
    return totals


def shards(queries, key_rows, value_rows, target, norm_gain, valid_mask):
    length, columns = queries.shape
    heads = columns // HEAD_DIM
    head_count = lax.axis_size("head")
    plan = Plan(length, heads, lax.axis_size("seq"), head_count)
    group, own = plan.group, plan.own
    product = 6 * HEAD_DIM**3 * heads
    seat = jnp.reshape(lax.axis_index("seq"), (1,)).astype(jnp.int32)
    gain = norm_gain.reshape(1, columns)
    mask = valid_mask.reshape(1, length)
    sum_shape = shape(plan.state_rows + TAIL, HEAD_DIM)
    state = shape(plan.state_rows, HEAD_DIM)
    piece = shape(plan.part_rows, HEAD_DIM)
    wide = shape(length, columns)
    bind = lambda kernel: functools.partial(kernel, plan)

    kv = call(
        bind(state_kernel),
        [sum_shape] * group,
        product,
        seat,
        in_hbm(key_rows),
        in_hbm(value_rows),
        in_hbm(mask),
        specs=[ANY, ANY, VMEM],
        scratch=[
            pltpu.VMEM((group, length, own * HEAD_DIM), f32),
            pltpu.VMEM((group, length, own * HEAD_DIM), f32),
            pltpu.SemaphoreType.DMA((2, group)),
        ],
    )
    scores, local, aim = call(
        bind(local_kernel),
        [shape(heads, length, length), wide, wide],
        2 * product,
        seat,
        queries,
        key_rows,
        value_rows,
        target,
        gain,
        mask,
    )
    kv = swap_all(kv, "seq")
    (total,) = call(bind(total_kernel), [sum_shape], 0, seat, *kv)
    totals = swap_totals(plan, total)
    priors = call(bind(prior_kernel), [state] * group, 0, seat, *kv, *totals[1:])
    priors = swap_all(priors, "seq")
    attended, stats = call(
        bind(attend_kernel),
        [wide, shape(TAIL, length)],
        product,
        seat,
        queries,
        local,
        aim,
        *priors,
    )
    stats = swap_all([stats] * head_count, "head")
    grad, *states = call(
        bind(grad_kernel),
        [wide] + [sum_shape] * group,
        product,
        seat,
        queries,
        attended,
        aim,
        *totals,
        *stats,
        scratch=[pltpu.VMEM((TAIL, length), f32)],
    )
    grad_query, part_key, part_value = call(
        bind(local_grad_kernel), [wide] * 3, 5 * product, seat, queries, key_rows, value_rows, grad, scores, *priors
    )
    states = swap_all(states, "seq")
    (grad_total,) = call(bind(total_kernel), [sum_shape], 0, seat, *states)
    grad_totals = swap_totals(plan, grad_total)
    *later, loss = call(
        bind(later_kernel),
        [state] * group + [shape(1, 1)],
        0,
        seat,
        *totals,
        *states,
        *grad_totals,
        part_key,
        specs=[VMEM] * (2 * len(totals) + group) + [ANY],
    )
    later = swap_all(later, "seq")
    grad_key, grad_value = call(
        bind(final_kernel), [wide] * 2, 2 * product, seat, key_rows, value_rows, part_key, part_value, *later
    )
    return (grad_query, grad_key, grad_value, loss[0, 0])


def solution(mesh):
    return jax.shard_map(
        shards,
        mesh=mesh,
        in_specs=(
            P("seq", "head"),
            P("seq", "head"),
            P("seq", "head"),
            P("seq", "head"),
            P("head"),
            P("seq"),
        ),
        out_specs=(P("seq", "head"), P("seq", "head"), P("seq", "head"), P()),
        check_vma=False,
    )
```

```python
import functools

import jax
import jax.numpy as jnp
from jax import lax
from jax.experimental import pallas as pl
from jax.experimental.pallas import tpu as pltpu
from jax.sharding import PartitionSpec as P

HEAD_DIM = 128
TAIL = 8
epsilon = 1e-06
f32 = jnp.float32
bf16 = jnp.bfloat16
SMEM = pl.BlockSpec(memory_space=pltpu.SMEM)
VMEM = pl.BlockSpec(memory_space=pltpu.VMEM)
ANY = pl.BlockSpec(memory_space=pl.ANY)

NN = ((1,), (0,))
NT = ((1,), (1,))
TN = ((0,), (0,))


def split(x):
    high = x.astype(bf16)
    return high, (x - high.astype(f32)).astype(bf16)


def dot(a, b, dims):
    ca, cb = dims[0][0], dims[1][0]
    left = jnp.concatenate(a, axis=ca)
    both = jnp.concatenate(b, axis=1 - cb)
    right = jnp.concatenate([both, both], axis=cb)
    out = lax.dot_general(left, right, (dims, ((), ())), preferred_element_type=f32)
    n = out.shape[1] // 2
    return out[:, :n] + out[:, n:]


def head_cols(h):
    return pl.ds(pl.multiple_of(h * HEAD_DIM, HEAD_DIM), HEAD_DIM)


def rows_of(i):
    return slice(i * HEAD_DIM, (i + 1) * HEAD_DIM)


def in_hbm(x):
    return pltpu.with_memory_space_constraint(x, pltpu.HBM)


def shape(*s):
    return jax.ShapeDtypeStruct(s, f32)


def call(kernel, outs, flops, seat, *args, specs=None, out_specs=None, scratch=(), aliases=None, limit=24):
    specs = specs or [VMEM] * len(args)
    place = [] if seat is None else [seat]
    nbytes = sum(a.size * 4 for a in args) + sum(o.size * 4 for o in outs)
    return pl.pallas_call(
        kernel,
        out_shape=outs,
        in_specs=[SMEM] * len(place) + specs,
        out_specs=out_specs or [VMEM] * len(outs),
        scratch_shapes=scratch,
        input_output_aliases=aliases or {},
        compiler_params=pltpu.CompilerParams(vmem_limit_bytes=limit * 1024 * 1024),
        cost_estimate=pl.CostEstimate(flops=flops, bytes_accessed=nbytes, transcendentals=0),
    )(*place, *args)


def causal_mask(n):
    return lax.broadcasted_iota(jnp.int32, (n, n), 0) >= lax.broadcasted_iota(jnp.int32, (n, n), 1)


def column(row, n):
    return jnp.broadcast_to(row, (n, n)).T


def pair_sum(parts):
    parts = list(parts)
    while len(parts) > 1:
        parts = [parts[i] + parts[i + 1] for i in range(0, len(parts), 2)]
    return parts[0]


class Plan:
    def __init__(self, length, heads, seq, head):
        group = 1
        while group < 4 and seq % (2 * group) == 0 and heads % (2 * group) == 0:
            group *= 2
        self.length, self.heads, self.head, self.group, self.own = length, heads, head, group, heads // group
        self.width, self.tokens = heads * HEAD_DIM * head, length * seq
        self.bits = [group << i for i in range(30) if group << i < seq]
        self.swaps = [bit | (bit // 2 if bit == group else 0) for bit in self.bits]
        self.state_rows = self.own * HEAD_DIM
        self.body = slice(0, self.state_rows)
        self.tail = slice(self.state_rows, self.state_rows + TAIL)

    def owned(self, seat, x):
        return (seat % self.group) ^ ((seat & self.group) // 2) ^ x

    def head_of(self, seat, x, i):
        return self.owned(seat, x) * self.own + i

    def share(self, seat, x, count=1):
        start = self.owned(seat, x) // count * (count * self.state_rows)
        return pl.ds(pl.multiple_of(start, HEAD_DIM), count * self.state_rows)


def outer_sum(plan, seat, reverse, totals):
    total = jnp.zeros((plan.state_rows, HEAD_DIM), f32)
    for bit, other in zip(plan.bits, totals):
        upper = (seat & bit) != 0
        counts = jnp.logical_not(upper) if reverse else upper
        total = total + jnp.where(counts, other[plan.body, :], 0.0)
    return total


def state_at(plan, seat, reverse, x, outer, parts):
    here = seat % plan.group
    total = outer
    for y in range(plan.group):
        if y != x:
            ahead = (here ^ y) > (here ^ x) if reverse else (here ^ y) < (here ^ x)
            total = total + jnp.where(ahead, parts[y][plan.body, :], 0.0)
    return total


def full_count(plan, totals):
    count = totals[0][plan.tail, :]
    for other in totals[1:]:
        count = count + other[plan.tail, :]
    return count[0:1, :]


def state_kernel(plan, k_hbm, v_hbm, mask_hbm, *refs):
    group = plan.group
    out, (k, v, mask, sems) = refs[:group], refs[group:]
    seat = [lax.axis_index("seq")]
    pair = min(group, 2)
    copies = {}
    for x in range(0, group, pair):
        cols = plan.share(seat[0], x, pair)
        copies[x] = [
            pltpu.make_async_copy(src.at[:, cols], dst.at[:, cols], sems.at[i, x])
            for i, (src, dst) in enumerate(((k_hbm, k), (v_hbm, v)))
        ]
        for copy in copies[x]:
            copy.start()
    mask_copy = pltpu.make_async_copy(mask_hbm, mask, sems.at[0, group])
    mask_copy.start()
    for x in range(group):
        for copy in copies.get(x, ()):
            copy.wait()
        for i in range(plan.own):
            cols = head_cols(plan.head_of(seat[0], x, i))
            out[x][rows_of(i), :] = dot(split(k[:, cols]), split(v[:, cols]), TN)
    mask_copy.wait()
    count = jnp.sum(mask[...].astype(f32))
    for x in range(group):
        out[x][plan.tail, :] = jnp.full((TAIL, HEAD_DIM), count, f32)


def local_kernel(plan, seat, q_hbm, k, v, target_hbm, gain, mask, q, scores, local, aim, target, sems):
    copies = [
        pltpu.make_async_copy(src, dst, sems.at[i]) for i, (src, dst) in enumerate(((q_hbm, q), (target_hbm, target)))
    ]
    for copy in copies:
        copy.start()
    causal = causal_mask(plan.length)
    valid = column(mask[...].astype(f32), plan.length)
    for copy in copies:
        copy.wait()
    for h in range(plan.heads):
        cols = head_cols(h)
        s = dot(split(q[:, cols]), split(k[:, cols]), NT)
        s = jnp.where(causal, s, 0.0)
        scores[h] = s
        local[:, cols] = dot(split(s), split(v[:, cols]), NN)
        aim[:, cols] = valid * (gain[:, cols] * target[:, cols])


def total_kernel(plan, seat, *refs):
    refs[-1][...] = pair_sum(r[...] for r in refs[: plan.group])


def prior_kernel(plan, seat, *refs):
    group = plan.group
    parts, totals, outs = refs[:group], refs[group : -group], refs[-group:]
    outer = outer_sum(plan, seat[0], False, totals)
    for x in range(group):
        outs[x][...] = state_at(plan, seat[0], False, x, outer, parts)


def attend_kernel(plan, which, last, seat, q, local, aim, *refs):
    n = len(which)
    priors, refs = refs[:n], refs[n:]
    if last:
        squares, dots = refs[0][...], refs[1][...]
        refs = refs[2:]
    else:
        squares = jnp.zeros((plan.length, HEAD_DIM), f32)
        dots = jnp.zeros((plan.length, HEAD_DIM), f32)
    attended, sums = refs[:n], refs[n:]
    for x, prior, out in zip(which, priors, attended):
        for i in range(plan.own):
            cols = head_cols(plan.head_of(seat[0], x, i))
            a = local[:, cols] + dot(split(q[:, cols]), split(prior[rows_of(i), :]), NN)
            out[:, rows_of(i)] = a
            squares = squares + a * a
            dots = dots + aim[:, cols] * a
    if last:
        (stats,) = sums
        stats[0:1, :] = jnp.sum(squares.T, axis=0, keepdims=True)
        stats[1:2, :] = jnp.sum(dots.T, axis=0, keepdims=True)
        stats[2:, :] = jnp.zeros((TAIL - 2, plan.length), f32)
    else:
        sums[0][...] = squares
        sums[1][...] = dots


def scales(plan, stats, row, count):
    squares, dots = stats[pl.ds(row, 1), :], stats[pl.ds(row + 1, 1), :]
    inverse_rms = lax.rsqrt(squares / plan.width + epsilon)
    left = (plan.tokens / count) * inverse_rms
    right = left * (inverse_rms * inverse_rms * dots / plan.width)
    return left, right, inverse_rms * dots


def grad_kernel(plan, seat, q, aim, *refs):
    refs = list(refs)
    take = lambda n: [refs.pop(0) for _ in range(n)]
    attended, totals, stat_parts = take(plan.group), take(1 + len(plan.swaps)), take(plan.head)
    (grad,), out = take(1), take(plan.group)
    (stats,) = refs
    stats[...] = pair_sum(r[...] for r in stat_parts)
    left, right, losses = scales(plan, stats, 0, full_count(plan, totals))
    left, right = column(left, plan.length), column(right, plan.length)
    loss = jnp.sum(losses)
    for x in range(plan.group):
        for i in range(plan.own):
            cols = head_cols(plan.head_of(seat[0], x, i))
            g = left * aim[:, cols] - right * attended[x][:, rows_of(i)]
            grad[:, cols] = g
            out[x][rows_of(i), :] = dot(split(q[:, cols]), split(g), TN)
        out[x][plan.tail, :] = jnp.full((TAIL, HEAD_DIM), loss, f32)


def local_grad_kernel(plan, seat, q, k, v, grad, scores, *refs):
    priors, (grad_q, grad_k, grad_v) = refs[: plan.group], refs[plan.group :]
    causal = causal_mask(plan.length)
    for x in range(plan.group):
        for i in range(plan.own):
            h = plan.head_of(seat[0], x, i)
            cols = head_cols(h)
            g = split(grad[:, cols])
            gs = split(jnp.where(causal, dot(g, split(v[:, cols]), NT), 0.0))
            prior = split(priors[x][rows_of(i), :])
            grad_q[:, cols] = dot(gs, split(k[:, cols]), NN) + dot(g, prior, NT)
            grad_k[:, cols] = dot(gs, split(q[:, cols]), TN)
            grad_v[:, cols] = dot(split(scores[h]), g, TN)


def later_kernel(plan, seat, *refs):
    group = plan.group
    states, totals, outs = refs[:group], refs[group : -group - 1], refs[-group:]
    outer = outer_sum(plan, seat[0], True, totals)
    for x in range(group):
        outs[x][...] = state_at(plan, seat[0], True, x, outer, states)


def loss_kernel(plan, seat, *refs):
    n = 1 + len(plan.swaps)
    refs[-1][...] = (full_count(plan, refs[n : 2 * n]) / full_count(plan, refs[:n]))[:, 0:1]


def final_kernel(plan, which, seat, k, v, part_k, part_v, *refs):
    n = len(which)
    later = refs[:n]
    grad_k, grad_v, block_k, block_v, sems = refs[-5:]
    copies = []
    for j, x in enumerate(which):
        for i in range(plan.own):
            cols = head_cols(plan.head_of(seat[0], x, i))
            state = split(later[j][rows_of(i), :])
            block_k[j, :, rows_of(i)] = part_k[:, cols] + dot(split(v[:, cols]), state, NT)
            block_v[j, :, rows_of(i)] = part_v[:, cols] + dot(split(k[:, cols]), state, NN)
        for m, (block, out) in enumerate(((block_k, grad_k), (block_v, grad_v))):
            copies.append(pltpu.make_async_copy(block.at[j], out.at[:, plan.share(seat[0], x)], sems.at[m, j]))
            copies[-1].start()
    for copy in copies:
        copy.wait()


def swap(value, axis, step):
    return lax.ppermute(value, axis, [(i, i ^ step) for i in range(lax.axis_size(axis))])


def swap_all(parts, axis):
    return [parts[0]] + [swap(part, axis, x) for x, part in enumerate(parts) if x]


def swap_totals(plan, total):
    totals = [total]
    for step in plan.swaps:
        totals.append(swap(total, "seq", step))
        if step != plan.swaps[-1]:
            total = total + totals[-1]
    return totals


def shards(queries, key_rows, value_rows, target, norm_gain, valid_mask):
    length, columns = queries.shape
    heads = columns // HEAD_DIM
    head_count = lax.axis_size("head")
    plan = Plan(length, heads, lax.axis_size("seq"), head_count)
    group, own = plan.group, plan.own
    product = 6 * HEAD_DIM**3 * heads
    seat = jnp.reshape(lax.axis_index("seq"), (1,)).astype(jnp.int32)
    gain = norm_gain.reshape(1, columns)
    mask = valid_mask.reshape(1, length)
    sum_shape = shape(plan.state_rows + TAIL, HEAD_DIM)
    state = shape(plan.state_rows, HEAD_DIM)
    piece = shape(length, plan.state_rows)
    wide = shape(length, columns)
    bind = lambda kernel: functools.partial(kernel, plan)

    *kv, key_rows, value_rows = call(
        bind(state_kernel),
        [sum_shape] * group + [wide] * 2,
        product,
        None,
        in_hbm(key_rows),
        in_hbm(value_rows),
        in_hbm(mask),
        specs=[ANY] * 3,
        scratch=[pltpu.VMEM((1, length), jnp.int32), pltpu.SemaphoreType.DMA((2, group + 1))],
    )
    queries, scores, local, aim = call(
        bind(local_kernel),
        [wide, shape(heads, length, length), wide, wide],
        2 * product,
        seat,
        in_hbm(queries),
        key_rows,
        value_rows,
        in_hbm(target),
        in_hbm(gain),
        in_hbm(mask),
        specs=[ANY, VMEM, VMEM, ANY, VMEM, VMEM],
        scratch=[pltpu.VMEM((length, columns), f32), pltpu.SemaphoreType.DMA((2,))],
    )
    kv = swap_all(kv, "seq")
    (total,) = call(bind(total_kernel), [sum_shape], 0, seat, *kv)
    totals = swap_totals(plan, total)
    priors = call(bind(prior_kernel), [state] * group, 0, seat, *kv, *totals[1:])
    priors = swap_all(priors, "seq")
    early, late = list(range(group - 1)), [group - 1]
    column_sum = shape(length, HEAD_DIM)
    *attended, squares, dots = call(
        functools.partial(attend_kernel, plan, early, False),
        [piece] * len(early) + [column_sum] * 2,
        product,
        seat,
        queries,
        local,
        aim,
        *priors[:-1],
    )
    last, stats = call(
        functools.partial(attend_kernel, plan, late, True),
        [piece, shape(TAIL, length)],
        product // group,
        seat,
        queries,
        local,
        aim,
        priors[-1],
        squares,
        dots,
    )
    attended.append(last)
    stats = swap_all([stats] * head_count, "head")
    grad, *states = call(
        bind(grad_kernel),
        [wide] + [sum_shape] * group,
        product,
        seat,
        queries,
        aim,
        *attended,
        *totals,
        *stats,
        scratch=[pltpu.VMEM((TAIL, length), f32)],
    )
    grad_query, part_key, part_value = call(
        bind(local_grad_kernel), [wide] * 3, 5 * product, seat, queries, key_rows, value_rows, grad, scores, *priors
    )
    states = swap_all(states, "seq")
    (grad_total,) = call(bind(total_kernel), [sum_shape], 0, seat, *states)
    grad_totals = swap_totals(plan, grad_total)
    later = call(
        bind(later_kernel),
        [state] * group,
        0,
        seat,
        *states,
        *grad_totals[1:],
        part_key,
        specs=[VMEM] * (group + len(plan.swaps)) + [ANY],
    )
    (loss,) = call(bind(loss_kernel), [shape(1, 1)], 0, seat, *totals, *grad_totals)
    later = swap_all(later, "seq")
    grads = []
    for which in [early[:2], *([x] for x in early[2:]), late]:
        block = pltpu.VMEM((len(which), length, plan.state_rows), f32)
        inputs = [key_rows, value_rows, part_key, part_value, *(later[x] for x in which)]
        grads = call(
            functools.partial(final_kernel, plan, which),
            [wide] * 2,
            2 * product * len(which) // group,
            seat,
            *inputs,
            *grads,
            specs=[VMEM] * len(inputs) + [ANY] * len(grads),
            out_specs=[ANY] * 2,
            scratch=[block, block, pltpu.SemaphoreType.DMA((2, len(which)))],
            aliases={1 + len(inputs) + i: i for i in range(len(grads))},
        )
    grad_key, grad_value = grads
    return (grad_query, grad_key, grad_value, loss[0, 0])


def solution(mesh):
    return jax.shard_map(
        shards,
        mesh=mesh,
        in_specs=(
            P("seq", "head"),
            P("seq", "head"),
            P("seq", "head"),
            P("seq", "head"),
            P("head"),
            P("seq"),
        ),
        out_specs=(P("seq", "head"), P("seq", "head"), P("seq", "head"), P()),
        check_vma=False,
    )
```

```python
import functools

import jax
import jax.numpy as jnp
from jax import lax
from jax.experimental import pallas as pl
from jax.experimental.pallas import tpu as pltpu
from jax.sharding import PartitionSpec as P

HEAD_DIM = 128
TAIL = 8
epsilon = 1e-06
f32 = jnp.float32
bf16 = jnp.bfloat16
SMEM = pl.BlockSpec(memory_space=pltpu.SMEM)
VMEM = pl.BlockSpec(memory_space=pltpu.VMEM)
ANY = pl.BlockSpec(memory_space=pl.ANY)

NN = ((1,), (0,))
NT = ((1,), (1,))
TN = ((0,), (0,))


def split(x):
    high = x.astype(bf16)
    return high, (x - high.astype(f32)).astype(bf16)


def dot(a, b, dims):
    ca, cb = dims[0][0], dims[1][0]
    left = jnp.concatenate(a, axis=ca)
    both = jnp.concatenate(b, axis=1 - cb)
    right = jnp.concatenate([both, both], axis=cb)
    out = lax.dot_general(left, right, (dims, ((), ())), preferred_element_type=f32)
    n = out.shape[1] // 2
    return out[:, :n] + out[:, n:]


def head_cols(h):
    return pl.ds(pl.multiple_of(h * HEAD_DIM, HEAD_DIM), HEAD_DIM)


def rows_of(i):
    return slice(i * HEAD_DIM, (i + 1) * HEAD_DIM)


def in_hbm(x):
    return pltpu.with_memory_space_constraint(x, pltpu.HBM)


def shape(*s):
    return jax.ShapeDtypeStruct(s, f32)


def call(kernel, outs, flops, seat, *args, specs=None, out_specs=None, scratch=(), aliases=None, limit=24):
    specs = specs or [VMEM] * len(args)
    place = [] if seat is None else [seat]
    nbytes = sum(a.size * 4 for a in args) + sum(o.size * 4 for o in outs)
    return pl.pallas_call(
        kernel,
        out_shape=outs,
        in_specs=[SMEM] * len(place) + specs,
        out_specs=out_specs or [VMEM] * len(outs),
        scratch_shapes=scratch,
        input_output_aliases=aliases or {},
        compiler_params=pltpu.CompilerParams(vmem_limit_bytes=limit * 1024 * 1024),
        cost_estimate=pl.CostEstimate(flops=flops, bytes_accessed=nbytes, transcendentals=0),
    )(*place, *args)


def causal_mask(n):
    return lax.broadcasted_iota(jnp.int32, (n, n), 0) >= lax.broadcasted_iota(jnp.int32, (n, n), 1)


def column(row, n):
    return jnp.broadcast_to(row, (n, n)).T


def pair_sum(parts):
    parts = list(parts)
    while len(parts) > 1:
        parts = [parts[i] + parts[i + 1] for i in range(0, len(parts), 2)]
    return parts[0]


class Plan:
    def __init__(self, length, heads, seq, head):
        group = 1
        while group < 4 and seq % (2 * group) == 0 and heads % (2 * group) == 0:
            group *= 2
        self.length, self.heads, self.head, self.group, self.own = length, heads, head, group, heads // group
        self.width, self.tokens = heads * HEAD_DIM * head, length * seq
        self.bits = [group << i for i in range(30) if group << i < seq]
        self.swaps = [bit | (bit // 2 if bit == group else 0) for bit in self.bits]
        self.state_rows = self.own * HEAD_DIM
        self.last = group // 2
        self.body = slice(0, self.state_rows)
        self.tail = slice(self.state_rows, self.state_rows + TAIL)

    def owned(self, seat, x):
        return (seat % self.group) ^ ((seat & self.group) // 2) ^ x

    def head_of(self, seat, x, i):
        return self.owned(seat, x) * self.own + i

    def share(self, seat, x, count=1):
        start = self.owned(seat, x) // count * (count * self.state_rows)
        return pl.ds(pl.multiple_of(start, HEAD_DIM), count * self.state_rows)


def outer_sum(plan, seat, reverse, totals):
    total = jnp.zeros((plan.state_rows, HEAD_DIM), f32)
    for bit, other in zip(plan.bits, totals):
        upper = (seat & bit) != 0
        counts = jnp.logical_not(upper) if reverse else upper
        total = total + jnp.where(counts, other[plan.body, :], 0.0)
    return total


def state_at(plan, seat, reverse, x, outer, parts):
    here = seat % plan.group
    total = outer
    for y in range(plan.group):
        if y != x:
            ahead = (here ^ y) > (here ^ x) if reverse else (here ^ y) < (here ^ x)
            total = total + jnp.where(ahead, parts[y][plan.body, :], 0.0)
    return total


def state_kernel(plan, k_hbm, v_hbm, *refs):
    group = plan.group
    out, (k, v, sems) = refs[:group], refs[group:]
    seat = lax.axis_index("seq")
    pair = min(group, 2)
    copies = {}
    for x in range(0, group, pair):
        cols = plan.share(seat, x, pair)
        copies[x] = [
            pltpu.make_async_copy(src.at[:, cols], dst.at[:, cols], sems.at[i, x])
            for i, (src, dst) in enumerate(((k_hbm, k), (v_hbm, v)))
        ]
        for copy in copies[x]:
            copy.start()
    for x in range(group):
        for copy in copies.get(x, ()):
            copy.wait()
        for i in range(plan.own):
            cols = head_cols(plan.head_of(seat, x, i))
            out[x][rows_of(i), :] = dot(split(k[:, cols]), split(v[:, cols]), TN)


def local_kernel(plan, seat, q_hbm, k, v, target_hbm, gain, mask, q, flipped, scores, local, aim, count, target, sems):
    copies = [
        pltpu.make_async_copy(src, dst, sems.at[i]) for i, (src, dst) in enumerate(((q_hbm, q), (target_hbm, target)))
    ]
    for copy in copies:
        copy.start()
    causal = causal_mask(plan.length)
    valid = mask[...].astype(f32)
    count[...] = jnp.full((TAIL, HEAD_DIM), jnp.sum(valid), f32)
    valid = column(valid, plan.length)
    for copy in copies:
        copy.wait()
    for h in range(plan.heads):
        cols = head_cols(h)
        flipped[h] = q[:, cols].T
        s = dot(split(q[:, cols]), split(k[:, cols]), NT)
        s = jnp.where(causal, s, 0.0)
        scores[h] = s
        local[:, cols] = dot(split(s), split(v[:, cols]), NN)
        aim[:, cols] = valid * (gain[:, cols] * target[:, cols])


def total_kernel(plan, seat, *refs):
    parts, out = refs[:-1], refs[-1]
    out[plan.body, :] = pair_sum(r[plan.body, :] for r in parts)
    if out.shape[0] > plan.state_rows:
        out[plan.tail, :] = parts[0][plan.tail, :] + parts[plan.last][plan.tail, :]


def prior_kernel(plan, seat, *refs):
    group = plan.group
    parts, totals, outs = refs[:group], refs[group : -group], refs[-group:]
    outer = outer_sum(plan, seat[0], False, totals)
    for x in range(group):
        outs[x][...] = state_at(plan, seat[0], False, x, outer, parts)


def attend_kernel(plan, which, last, seat, q, local, aim, *refs):
    n = len(which)
    priors, refs = refs[:n], refs[n:]
    if last:
        squares, dots = refs[0][...], refs[1][...]
        refs = refs[2:]
    else:
        squares = jnp.zeros((plan.length, HEAD_DIM), f32)
        dots = jnp.zeros((plan.length, HEAD_DIM), f32)
    attended, sums = refs[:n], refs[n:]
    for x, prior, out in zip(which, priors, attended):
        for i in range(plan.own):
            cols = head_cols(plan.head_of(seat[0], x, i))
            a = local[:, cols] + dot(split(q[:, cols]), split(prior[rows_of(i), :]), NN)
            out[:, rows_of(i)] = a
            squares = squares + a * a
            dots = dots + aim[:, cols] * a
    if last:
        (stats,) = sums
        stats[0:1, :] = jnp.sum(squares.T, axis=0, keepdims=True)
        stats[1:2, :] = jnp.sum(dots.T, axis=0, keepdims=True)
        stats[2:, :] = jnp.zeros((TAIL - 2, plan.length), f32)
    else:
        sums[0][...] = squares
        sums[1][...] = dots


def scales(plan, stats):
    squares, dots = stats[0:1, :], stats[1:2, :]
    inverse_rms = lax.rsqrt(squares / plan.width + epsilon)
    loss = inverse_rms * dots
    return inverse_rms, inverse_rms * inverse_rms * loss / plan.width, loss


def grad_kernel(plan, seat, flipped, aim, count, *refs):
    refs = list(refs)
    take = lambda n: [refs.pop(0) for _ in range(n)]
    attended, stat_parts, (grad,), out = take(plan.group), take(plan.head), take(1), take(plan.group)
    left, right, losses = scales(plan, pair_sum(r[...] for r in stat_parts))
    left, right = column(left, plan.length), column(right, plan.length)
    row = lax.broadcasted_iota(jnp.int32, (TAIL, HEAD_DIM), 0)
    tail = jnp.where(row == 0, jnp.sum(losses), count[...])
    for x in range(plan.group):
        for i in range(plan.own):
            h = plan.head_of(seat[0], x, i)
            cols = head_cols(h)
            g = left * aim[:, cols] - right * attended[x][:, rows_of(i)]
            grad[:, cols] = g
            out[x][rows_of(i), :] = dot(split(flipped[h]), split(g), NN)
        if x in (0, plan.last):
            out[x][plan.tail, :] = tail


def local_grad_kernel(plan, seat, q, k, v, grad, scores, *refs):
    priors, (grad_q, grad_k, grad_v) = refs[: plan.group], refs[plan.group :]
    causal = causal_mask(plan.length)
    for x in range(plan.group):
        for i in range(plan.own):
            h = plan.head_of(seat[0], x, i)
            cols = head_cols(h)
            g = split(grad[:, cols])
            gs = split(jnp.where(causal, dot(g, split(v[:, cols]), NT), 0.0))
            prior = split(priors[x][rows_of(i), :])
            grad_q[:, cols] = dot(gs, split(k[:, cols]), NN) + dot(g, prior, NT)
            grad_k[:, cols] = dot(gs, split(q[:, cols]), TN)
            grad_v[:, cols] = dot(split(scores[h]), g, TN)


def later_kernel(plan, seat, *refs):
    group = plan.group
    states, totals, outs = refs[:group], refs[group : -group - 1], refs[-group:]
    outer = outer_sum(plan, seat[0], True, totals[1:])
    tail = totals[0][plan.tail, :]
    for other in totals[1:]:
        tail = tail + other[plan.tail, :]
    for x in range(group):
        outs[x][plan.body, :] = state_at(plan, seat[0], True, x, outer, states)
        if x == min(1, group - 1):
            outs[x][plan.tail, :] = tail


def final_kernel(plan, which, seat, k, v, part_k, part_v, sent, *refs):
    n = len(which)
    first = which[0] == 0
    later, refs = list(refs[:n]), refs[n:]
    if first:
        (part_q, loss, grad_q, grad_k, grad_v, block_k, block_v, block_q, sems) = refs
        tail = later[-1][plan.tail, :]
    else:
        (tail_ref, _, _, grad_k, grad_v, block_k, block_v, sems) = refs
        tail = tail_ref[plan.tail, :]
    if plan.group > 1:
        tail = sent[plan.tail, :] + tail
    factor = plan.tokens / tail[1:2, 0:1]
    copies = []
    for j, x in enumerate(which):
        for i in range(plan.own):
            cols = head_cols(plan.head_of(seat[0], x, i))
            state = split(later[j][rows_of(i), :])
            block_k[j, :, rows_of(i)] = factor * (part_k[:, cols] + dot(split(v[:, cols]), state, NT))
            block_v[j, :, rows_of(i)] = factor * (part_v[:, cols] + dot(split(k[:, cols]), state, NN))
        for m, (block, out) in enumerate(((block_k, grad_k), (block_v, grad_v))):
            copies.append(pltpu.make_async_copy(block.at[j], out.at[:, plan.share(seat[0], x)], sems.at[m, j]))
            copies[-1].start()
    if first:
        block_q[...] = factor * part_q[...]
        copies.append(pltpu.make_async_copy(block_q, grad_q, sems.at[2, 0]))
        copies[-1].start()
        loss[...] = tail[0:1, 0:1] / tail[1:2, 0:1]
    for copy in copies:
        copy.wait()


def swap(value, axis, step):
    return lax.ppermute(value, axis, [(i, i ^ step) for i in range(lax.axis_size(axis))])


def swap_all(parts, axis):
    return [parts[0]] + [swap(part, axis, x) for x, part in enumerate(parts) if x]


def swap_totals(plan, total):
    totals = [total]
    for step in plan.swaps:
        totals.append(swap(total, "seq", step))
        if step != plan.swaps[-1]:
            total = total + totals[-1]
    return totals


def shards(queries, key_rows, value_rows, target, norm_gain, valid_mask):
    length, columns = queries.shape
    heads = columns // HEAD_DIM
    head_count = lax.axis_size("head")
    plan = Plan(length, heads, lax.axis_size("seq"), head_count)
    group, own = plan.group, plan.own
    product = 6 * HEAD_DIM**3 * heads
    seat = jnp.reshape(lax.axis_index("seq"), (1,)).astype(jnp.int32)
    gain = norm_gain.reshape(1, columns)
    mask = valid_mask.reshape(1, length)
    sum_shape = shape(plan.state_rows + TAIL, HEAD_DIM)
    state = shape(plan.state_rows, HEAD_DIM)
    piece = shape(length, plan.state_rows)
    wide = shape(length, columns)
    bind = lambda kernel: functools.partial(kernel, plan)

    *kv, key_rows, value_rows = call(
        bind(state_kernel),
        [state] * group + [wide] * 2,
        product,
        None,
        in_hbm(key_rows),
        in_hbm(value_rows),
        specs=[ANY] * 2,
        scratch=[pltpu.SemaphoreType.DMA((2, group))],
    )
    queries, flipped, scores, local, aim, count = call(
        bind(local_kernel),
        [wide, shape(heads, HEAD_DIM, length), shape(heads, length, length), wide, wide, shape(TAIL, HEAD_DIM)],
        2 * product,
        seat,
        in_hbm(queries),
        key_rows,
        value_rows,
        in_hbm(target),
        in_hbm(gain),
        in_hbm(mask),
        specs=[ANY, VMEM, VMEM, ANY, VMEM, VMEM],
        scratch=[pltpu.VMEM((length, columns), f32), pltpu.SemaphoreType.DMA((2,))],
    )
    kv = swap_all(kv, "seq")
    (total,) = call(bind(total_kernel), [state], 0, seat, *kv)
    totals = swap_totals(plan, total)
    priors = call(bind(prior_kernel), [state] * group, 0, seat, *kv, *totals[1:])
    priors = swap_all(priors, "seq")
    early, late = list(range(group - 1)), [group - 1]
    column_sum = shape(length, HEAD_DIM)
    *attended, squares, dots = call(
        functools.partial(attend_kernel, plan, early, False),
        [piece] * len(early) + [column_sum] * 2,
        product,
        seat,
        queries,
        local,
        aim,
        *priors[:-1],
    )
    last, stats = call(
        functools.partial(attend_kernel, plan, late, True),
        [piece, shape(TAIL, length)],
        product // group,
        seat,
        queries,
        local,
        aim,
        priors[-1],
        squares,
        dots,
    )
    attended.append(last)
    stats = swap_all([stats] * head_count, "head")
    grad, *states = call(
        bind(grad_kernel),
        [wide] + [sum_shape if x in (0, plan.last) else state for x in range(group)],
        product,
        seat,
        flipped,
        aim,
        count,
        *attended,
        *stats,
    )
    part_query, part_key, part_value = call(
        bind(local_grad_kernel), [wide] * 3, 5 * product, seat, queries, key_rows, value_rows, grad, scores, *priors
    )
    states = swap_all(states, "seq")
    (grad_total,) = call(bind(total_kernel), [sum_shape], 0, seat, *states)
    grad_totals = swap_totals(plan, grad_total)
    later = call(
        bind(later_kernel),
        [sum_shape if x == min(1, group - 1) else state for x in range(group)],
        0,
        seat,
        *states,
        *grad_totals,
        part_key,
        specs=[VMEM] * (group + len(grad_totals)) + [ANY],
    )
    sent = later[min(1, group - 1)]
    later = swap_all(later, "seq")
    grads = []
    for which in [early[:2], *([x] for x in early[2:]), late]:
        block = pltpu.VMEM((len(which), length, plan.state_rows), f32)
        inputs = [key_rows, value_rows, part_key, part_value, sent, *(later[x] for x in which)]
        if not grads:
            loss, grad_query, *grads = call(
                functools.partial(final_kernel, plan, which),
                [shape(1, 1), wide, wide, wide],
                2 * product * len(which) // group,
                seat,
                *inputs,
                part_query,
                out_specs=[VMEM] + [ANY] * 3,
                scratch=[block, block, pltpu.VMEM((length, columns), f32), pltpu.SemaphoreType.DMA((3, len(which)))],
            )
            continue
        inputs.append(later[1])
        grads = call(
            functools.partial(final_kernel, plan, which),
            [wide] * 2,
            2 * product * len(which) // group,
            seat,
            *inputs,
            *grads,
            specs=[VMEM] * len(inputs) + [ANY] * 2,
            out_specs=[ANY] * 2,
            scratch=[block, block, pltpu.SemaphoreType.DMA((2, len(which)))],
            aliases={1 + len(inputs) + i: i for i in range(2)},
        )
    grad_key, grad_value = grads
    return (grad_query, grad_key, grad_value, loss[0, 0])


def solution(mesh):
    return jax.shard_map(
        shards,
        mesh=mesh,
        in_specs=(
            P("seq", "head"),
            P("seq", "head"),
            P("seq", "head"),
            P("seq", "head"),
            P("head"),
            P("seq"),
        ),
        out_specs=(P("seq", "head"), P("seq", "head"), P("seq", "head"), P()),
        check_vma=False,
    )
```

```python
import functools

import jax
import jax.numpy as jnp
from jax import lax
from jax.experimental import pallas as pl
from jax.experimental.pallas import tpu as pltpu
from jax.sharding import PartitionSpec as P

HEAD_DIM = 128
TAIL = 8
epsilon = 1e-06
f32 = jnp.float32
bf16 = jnp.bfloat16
SMEM = pl.BlockSpec(memory_space=pltpu.SMEM)
VMEM = pl.BlockSpec(memory_space=pltpu.VMEM)
ANY = pl.BlockSpec(memory_space=pl.ANY)

NN = ((1,), (0,))
NT = ((1,), (1,))
TN = ((0,), (0,))


def split(x):
    high = x.astype(bf16)
    return high, (x - high.astype(f32)).astype(bf16)


def dot(a, b, dims):
    ca, cb = dims[0][0], dims[1][0]
    left = jnp.concatenate(a, axis=ca)
    both = jnp.concatenate(b, axis=1 - cb)
    right = jnp.concatenate([both, both], axis=cb)
    out = lax.dot_general(left, right, (dims, ((), ())), preferred_element_type=f32)
    n = out.shape[1] // 2
    return out[:, :n] + out[:, n:]


def head_cols(h):
    return pl.ds(pl.multiple_of(h * HEAD_DIM, HEAD_DIM), HEAD_DIM)


def rows_of(i):
    return slice(i * HEAD_DIM, (i + 1) * HEAD_DIM)


def in_hbm(x):
    return pltpu.with_memory_space_constraint(x, pltpu.HBM)


def shape(*s):
    return jax.ShapeDtypeStruct(s, f32)


def call(kernel, outs, flops, seat, *args, specs=None, out_specs=None, scratch=(), aliases=None, limit=24):
    specs = specs or [VMEM] * len(args)
    place = [] if seat is None else [seat]
    nbytes = sum(a.size * 4 for a in args) + sum(o.size * 4 for o in outs)
    return pl.pallas_call(
        kernel,
        out_shape=outs,
        in_specs=[SMEM] * len(place) + specs,
        out_specs=out_specs or [VMEM] * len(outs),
        scratch_shapes=scratch,
        input_output_aliases=aliases or {},
        compiler_params=pltpu.CompilerParams(vmem_limit_bytes=limit * 1024 * 1024),
        cost_estimate=pl.CostEstimate(flops=flops, bytes_accessed=nbytes, transcendentals=0),
    )(*place, *args)


def causal_mask(n):
    return lax.broadcasted_iota(jnp.int32, (n, n), 0) >= lax.broadcasted_iota(jnp.int32, (n, n), 1)


def column(row, n):
    return jnp.broadcast_to(row, (HEAD_DIM, n)).T


def pair_sum(parts):
    parts = list(parts)
    while len(parts) > 1:
        parts = [parts[i] + parts[i + 1] for i in range(0, len(parts), 2)]
    return parts[0]


class Plan:
    def __init__(self, length, heads, seq, head):
        group = 1
        while group < 4 and seq % (2 * group) == 0 and heads % (2 * group) == 0:
            group *= 2
        self.length, self.heads, self.head, self.group, self.own = length, heads, head, group, heads // group
        self.width, self.tokens = heads * HEAD_DIM * head, length * seq
        self.bits = [group << i for i in range(30) if group << i < seq]
        self.swaps = [bit | (bit // 2 if bit == group else 0) for bit in self.bits]
        self.state_rows = self.own * HEAD_DIM
        self.last = group // 2
        self.body = slice(0, self.state_rows)
        self.tail = slice(self.state_rows, self.state_rows + TAIL)

    def owned(self, seat, x):
        return (seat % self.group) ^ ((seat & self.group) // 2) ^ x

    def head_of(self, seat, x, i):
        return self.owned(seat, x) * self.own + i

    def share(self, seat, x, count=1):
        start = self.owned(seat, x) // count * (count * self.state_rows)
        return pl.ds(pl.multiple_of(start, HEAD_DIM), count * self.state_rows)


def outer_sum(plan, seat, reverse, totals):
    total = jnp.zeros((plan.state_rows, HEAD_DIM), f32)
    for bit, other in zip(plan.bits, totals):
        upper = (seat & bit) != 0
        counts = jnp.logical_not(upper) if reverse else upper
        total = total + jnp.where(counts, other[plan.body, :], 0.0)
    return total


def state_at(plan, seat, reverse, x, outer, parts):
    here = seat % plan.group
    total = outer
    for y in range(plan.group):
        if y != x:
            ahead = (here ^ y) > (here ^ x) if reverse else (here ^ y) < (here ^ x)
            total = total + jnp.where(ahead, parts[y][plan.body, :], 0.0)
    return total


def state_kernel(plan, k_hbm, v_hbm, *refs):
    group = plan.group
    out, (k, v, sems) = refs[:group], refs[group:]
    seat = lax.axis_index("seq")
    pair = min(group, 2)
    copies = {}
    for x in range(0, group, pair):
        cols = plan.share(seat, x, pair)
        copies[x] = [
            pltpu.make_async_copy(src.at[:, cols], dst.at[:, cols], sems.at[i, x])
            for i, (src, dst) in enumerate(((k_hbm, k), (v_hbm, v)))
        ]
        for copy in copies[x]:
            copy.start()
    for x in range(group):
        for copy in copies.get(x, ()):
            copy.wait()
        for i in range(plan.own):
            cols = head_cols(plan.head_of(seat, x, i))
            out[x][rows_of(i), :] = dot(split(k[:, cols]), split(v[:, cols]), TN)


def local_kernel(plan, seat, q_hbm, k, v, target_hbm, gain, mask, q, flipped, scores, local, aim, count, target, sems):
    copies = [
        pltpu.make_async_copy(src, dst, sems.at[i]) for i, (src, dst) in enumerate(((q_hbm, q), (target_hbm, target)))
    ]
    for copy in copies:
        copy.start()
    causal = causal_mask(plan.length)
    valid = mask[...].astype(f32)
    count[...] = jnp.full((TAIL, HEAD_DIM), jnp.sum(valid), f32)
    valid = column(valid, plan.length)
    for copy in copies:
        copy.wait()
    for h in range(plan.heads):
        cols = head_cols(h)
        flipped[h] = q[:, cols].T
        s = dot(split(q[:, cols]), split(k[:, cols]), NT)
        s = jnp.where(causal, s, 0.0)
        scores[h] = s
        local[:, cols] = dot(split(s), split(v[:, cols]), NN)
        aim[:, cols] = valid * (gain[:, cols] * target[:, cols])


def total_kernel(plan, seat, *refs):
    parts, out = refs[:-1], refs[-1]
    out[plan.body, :] = pair_sum(r[plan.body, :] for r in parts)
    if out.shape[0] > plan.state_rows:
        out[plan.tail, :] = parts[0][plan.tail, :] + parts[plan.last][plan.tail, :]


def prior_kernel(plan, seat, *refs):
    group = plan.group
    parts, totals, outs = refs[:group], refs[group : -group], refs[-group:]
    outer = outer_sum(plan, seat[0], False, totals)
    for x in range(group):
        outs[x][...] = state_at(plan, seat[0], False, x, outer, parts)


def attend_kernel(plan, which, last, seat, q, local, aim, *refs):
    n = len(which)
    priors, refs = refs[:n], refs[n:]
    if last:
        squares, dots = refs[0][...], refs[1][...]
        refs = refs[2:]
    else:
        squares = jnp.zeros((plan.length, HEAD_DIM), f32)
        dots = jnp.zeros((plan.length, HEAD_DIM), f32)
    attended, sums = refs[:n], refs[n:]
    for x, prior, out in zip(which, priors, attended):
        for i in range(plan.own):
            cols = head_cols(plan.head_of(seat[0], x, i))
            a = local[:, cols] + dot(split(q[:, cols]), split(prior[rows_of(i), :]), NN)
            out[:, rows_of(i)] = a
            squares = squares + a * a
            dots = dots + aim[:, cols] * a
    if last:
        (stats,) = sums
        stats[0:1, :] = jnp.sum(squares.T, axis=0, keepdims=True)
        stats[1:2, :] = jnp.sum(dots.T, axis=0, keepdims=True)
        stats[2:, :] = jnp.zeros((TAIL - 2, plan.length), f32)
    else:
        sums[0][...] = squares
        sums[1][...] = dots


def scales(plan, stats):
    squares, dots = stats[0:1, :], stats[1:2, :]
    inverse_rms = lax.rsqrt(squares / plan.width + epsilon)
    loss = inverse_rms * dots
    return inverse_rms, inverse_rms * inverse_rms * loss / plan.width, loss


def grad_kernel(plan, seat, flipped, aim, count, *refs):
    refs = list(refs)
    take = lambda n: [refs.pop(0) for _ in range(n)]
    attended, stat_parts, (grad,), out = take(plan.group), take(plan.head), take(1), take(plan.group)
    left, right, losses = scales(plan, pair_sum(r[...] for r in stat_parts))
    left, right = column(left, plan.length), column(right, plan.length)
    row = lax.broadcasted_iota(jnp.int32, (TAIL, HEAD_DIM), 0)
    tail = jnp.where(row == 0, jnp.sum(losses), count[...])
    for x in range(plan.group):
        for i in range(plan.own):
            h = plan.head_of(seat[0], x, i)
            cols = head_cols(h)
            g = left * aim[:, cols] - right * attended[x][:, rows_of(i)]
            grad[:, cols] = g
            out[x][rows_of(i), :] = dot(split(flipped[h]), split(g), NN)
        if x in (0, plan.last):
            out[x][plan.tail, :] = tail


def local_grad_kernel(plan, seat, q, k, v, grad, scores, *refs):
    priors, (grad_q, grad_k, grad_v) = refs[: plan.group], refs[plan.group :]
    causal = causal_mask(plan.length)
    for x in range(plan.group):
        for i in range(plan.own):
            h = plan.head_of(seat[0], x, i)
            cols = head_cols(h)
            g = split(grad[:, cols])
            gs = split(jnp.where(causal, dot(g, split(v[:, cols]), NT), 0.0))
            prior = split(priors[x][rows_of(i), :])
            grad_q[:, cols] = dot(gs, split(k[:, cols]), NN) + dot(g, prior, NT)
            grad_k[:, cols] = dot(gs, split(q[:, cols]), TN)
            grad_v[:, cols] = dot(split(scores[h]), g, TN)


def later_kernel(plan, seat, *refs):
    group = plan.group
    states, totals, outs = refs[:group], refs[group : -group - 1], refs[-group:]
    outer = outer_sum(plan, seat[0], True, totals[1:])
    tail = totals[0][plan.tail, :]
    for other in totals[1:]:
        tail = tail + other[plan.tail, :]
    for x in range(group):
        outs[x][plan.body, :] = state_at(plan, seat[0], True, x, outer, states)
        if x == min(1, group - 1):
            outs[x][plan.tail, :] = tail


def final_kernel(plan, which, seat, k, v, part_k, part_v, sent, *refs):
    n = len(which)
    first = which[0] == 0
    later, refs = list(refs[:n]), refs[n:]
    if first:
        (part_q, loss, grad_q, grad_k, grad_v, block_k, block_v, block_q, sems) = refs
        tail = later[-1][plan.tail, :]
    else:
        (tail_ref, _, _, grad_k, grad_v, block_k, block_v, sems) = refs
        tail = tail_ref[plan.tail, :]
    if plan.group > 1:
        tail = sent[plan.tail, :] + tail
    factor = plan.tokens / tail[1:2, 0:1]
    copies = []
    for j, x in enumerate(which):
        for i in range(plan.own):
            cols = head_cols(plan.head_of(seat[0], x, i))
            state = split(later[j][rows_of(i), :])
            block_k[j, :, rows_of(i)] = factor * (part_k[:, cols] + dot(split(v[:, cols]), state, NT))
            block_v[j, :, rows_of(i)] = factor * (part_v[:, cols] + dot(split(k[:, cols]), state, NN))
        for m, (block, out) in enumerate(((block_k, grad_k), (block_v, grad_v))):
            copies.append(pltpu.make_async_copy(block.at[j], out.at[:, plan.share(seat[0], x)], sems.at[m, j]))
            copies[-1].start()
    if first:
        block_q[...] = factor * part_q[...]
        copies.append(pltpu.make_async_copy(block_q, grad_q, sems.at[2, 0]))
        copies[-1].start()
        loss[...] = tail[0:1, 0:1] / tail[1:2, 0:1]
    for copy in copies:
        copy.wait()


def swap(value, axis, step):
    return lax.ppermute(value, axis, [(i, i ^ step) for i in range(lax.axis_size(axis))])


def swap_all(parts, axis):
    return [parts[0]] + [swap(part, axis, x) for x, part in enumerate(parts) if x]


def swap_totals(plan, total):
    totals = [total]
    for step in plan.swaps:
        totals.append(swap(total, "seq", step))
        if step != plan.swaps[-1]:
            total = total + totals[-1]
    return totals


def shards(queries, key_rows, value_rows, target, norm_gain, valid_mask):
    length, columns = queries.shape
    heads = columns // HEAD_DIM
    head_count = lax.axis_size("head")
    plan = Plan(length, heads, lax.axis_size("seq"), head_count)
    group, own = plan.group, plan.own
    product = 6 * HEAD_DIM**3 * heads
    seat = jnp.reshape(lax.axis_index("seq"), (1,)).astype(jnp.int32)
    gain = norm_gain.reshape(1, columns)
    mask = valid_mask.reshape(1, length)
    sum_shape = shape(plan.state_rows + TAIL, HEAD_DIM)
    state = shape(plan.state_rows, HEAD_DIM)
    piece = shape(length, plan.state_rows)
    wide = shape(length, columns)
    bind = lambda kernel: functools.partial(kernel, plan)

    *kv, key_rows, value_rows = call(
        bind(state_kernel),
        [state] * group + [wide] * 2,
        product,
        None,
        in_hbm(key_rows),
        in_hbm(value_rows),
        specs=[ANY] * 2,
        scratch=[pltpu.SemaphoreType.DMA((2, group))],
    )
    queries, flipped, scores, local, aim, count = call(
        bind(local_kernel),
        [wide, shape(heads, HEAD_DIM, length), shape(heads, length, length), wide, wide, shape(TAIL, HEAD_DIM)],
        2 * product,
        seat,
        in_hbm(queries),
        key_rows,
        value_rows,
        in_hbm(target),
        in_hbm(gain),
        in_hbm(mask),
        specs=[ANY, VMEM, VMEM, ANY, VMEM, VMEM],
        scratch=[pltpu.VMEM((length, columns), f32), pltpu.SemaphoreType.DMA((2,))],
    )
    kv = swap_all(kv, "seq")
    (total,) = call(bind(total_kernel), [state], 0, seat, *kv)
    totals = swap_totals(plan, total)
    priors = call(bind(prior_kernel), [state] * group, 0, seat, *kv, *totals[1:])
    priors = swap_all(priors, "seq")
    early, late = list(range(group - 1)), [group - 1]
    column_sum = shape(length, HEAD_DIM)
    *attended, squares, dots = call(
        functools.partial(attend_kernel, plan, early, False),
        [piece] * len(early) + [column_sum] * 2,
        product,
        seat,
        queries,
        local,
        aim,
        *priors[:-1],
    )
    last, stats = call(
        functools.partial(attend_kernel, plan, late, True),
        [piece, shape(TAIL, length)],
        product // group,
        seat,
        queries,
        local,
        aim,
        priors[-1],
        squares,
        dots,
    )
    attended.append(last)
    stats = swap_all([stats] * head_count, "head")
    grad, *states = call(
        bind(grad_kernel),
        [wide] + [sum_shape if x in (0, plan.last) else state for x in range(group)],
        product,
        seat,
        flipped,
        aim,
        count,
        *attended,
        *stats,
    )
    part_query, part_key, part_value = call(
        bind(local_grad_kernel), [wide] * 3, 5 * product, seat, queries, key_rows, value_rows, grad, scores, *priors
    )
    states = swap_all(states, "seq")
    (grad_total,) = call(bind(total_kernel), [sum_shape], 0, seat, *states)
    grad_totals = swap_totals(plan, grad_total)
    later = call(
        bind(later_kernel),
        [sum_shape if x == min(1, group - 1) else state for x in range(group)],
        0,
        seat,
        *states,
        *grad_totals,
        part_key,
        specs=[VMEM] * (group + len(grad_totals)) + [ANY],
    )
    sent = later[min(1, group - 1)]
    later = swap_all(later, "seq")
    grads = []
    for which in [early[:2], *([x] for x in early[2:]), late]:
        block = pltpu.VMEM((len(which), length, plan.state_rows), f32)
        inputs = [key_rows, value_rows, part_key, part_value, sent, *(later[x] for x in which)]
        if not grads:
            loss, grad_query, *grads = call(
                functools.partial(final_kernel, plan, which),
                [shape(1, 1), wide, wide, wide],
                2 * product * len(which) // group,
                seat,
                *inputs,
                part_query,
                out_specs=[VMEM] + [ANY] * 3,
                scratch=[block, block, pltpu.VMEM((length, columns), f32), pltpu.SemaphoreType.DMA((3, len(which)))],
            )
            continue
        inputs.append(later[1])
        grads = call(
            functools.partial(final_kernel, plan, which),
            [wide] * 2,
            2 * product * len(which) // group,
            seat,
            *inputs,
            *grads,
            specs=[VMEM] * len(inputs) + [ANY] * 2,
            out_specs=[ANY] * 2,
            scratch=[block, block, pltpu.SemaphoreType.DMA((2, len(which)))],
            aliases={1 + len(inputs) + i: i for i in range(2)},
        )
    grad_key, grad_value = grads
    return (grad_query, grad_key, grad_value, loss[0, 0])


def solution(mesh):
    return jax.shard_map(
        shards,
        mesh=mesh,
        in_specs=(
            P("seq", "head"),
            P("seq", "head"),
            P("seq", "head"),
            P("seq", "head"),
            P("head"),
            P("seq"),
        ),
        out_specs=(P("seq", "head"), P("seq", "head"), P("seq", "head"), P()),
        check_vma=False,
    )
```

```python
import functools

import jax
import jax.numpy as jnp
from jax import lax
from jax.experimental import pallas as pl
from jax.experimental.pallas import tpu as pltpu
from jax.sharding import PartitionSpec as P

HEAD_DIM = 128
TAIL = 8
epsilon = 1e-06
f32 = jnp.float32
bf16 = jnp.bfloat16
SMEM = pl.BlockSpec(memory_space=pltpu.SMEM)
VMEM = pl.BlockSpec(memory_space=pltpu.VMEM)
ANY = pl.BlockSpec(memory_space=pl.ANY)

NN = ((1,), (0,))
NT = ((1,), (1,))
TN = ((0,), (0,))


def split(x):
    high = x.astype(bf16)
    return high, (x - high.astype(f32)).astype(bf16)


def dot(a, b, dims):
    ca, cb = dims[0][0], dims[1][0]
    left = jnp.concatenate(a, axis=ca)
    both = jnp.concatenate(b, axis=1 - cb)
    right = jnp.concatenate([both, both], axis=cb)
    out = lax.dot_general(left, right, (dims, ((), ())), preferred_element_type=f32)
    n = out.shape[1] // 2
    return out[:, :n] + out[:, n:]


def head_cols(h):
    return pl.ds(pl.multiple_of(h * HEAD_DIM, HEAD_DIM), HEAD_DIM)


def rows_of(i):
    return slice(i * HEAD_DIM, (i + 1) * HEAD_DIM)


def in_hbm(x):
    return pltpu.with_memory_space_constraint(x, pltpu.HBM)


def shape(*s):
    return jax.ShapeDtypeStruct(s, f32)


def call(kernel, outs, flops, seat, *args, specs=None, out_specs=None, scratch=(), aliases=None, limit=24):
    specs = specs or [VMEM] * len(args)
    place = [] if seat is None else [seat]
    nbytes = sum(a.size * 4 for a in args) + sum(o.size * 4 for o in outs)
    return pl.pallas_call(
        kernel,
        out_shape=outs,
        in_specs=[SMEM] * len(place) + specs,
        out_specs=out_specs or [VMEM] * len(outs),
        scratch_shapes=scratch,
        input_output_aliases=aliases or {},
        compiler_params=pltpu.CompilerParams(vmem_limit_bytes=limit * 1024 * 1024),
        cost_estimate=pl.CostEstimate(flops=flops, bytes_accessed=nbytes, transcendentals=0),
    )(*place, *args)


def causal_mask(n):
    return lax.broadcasted_iota(jnp.int32, (n, n), 0) >= lax.broadcasted_iota(jnp.int32, (n, n), 1)


def column(row, n):
    return jnp.broadcast_to(row, (HEAD_DIM, n)).T


def pair_sum(parts):
    parts = list(parts)
    while len(parts) > 1:
        parts = [parts[i] + parts[i + 1] for i in range(0, len(parts), 2)]
    return parts[0]


class Plan:
    def __init__(self, length, heads, seq, head):
        group = 1
        while group < 4 and seq % (2 * group) == 0 and heads % (2 * group) == 0:
            group *= 2
        self.length, self.heads, self.head, self.group, self.own = length, heads, head, group, heads // group
        self.width, self.tokens = heads * HEAD_DIM * head, length * seq
        self.bits = [group << i for i in range(30) if group << i < seq]
        self.swaps = [bit | (bit // 2 if bit == group else 0) for bit in self.bits]
        self.state_rows = self.own * HEAD_DIM
        self.last = group // 2
        self.body = slice(0, self.state_rows)
        self.tail = slice(self.state_rows, self.state_rows + TAIL)

    def owned(self, seat, x):
        return (seat % self.group) ^ ((seat & self.group) // 2) ^ x

    def head_of(self, seat, x, i):
        return self.owned(seat, x) * self.own + i

    def share(self, seat, x, count=1):
        start = self.owned(seat, x) // count * (count * self.state_rows)
        return pl.ds(pl.multiple_of(start, HEAD_DIM), count * self.state_rows)


def outer_sum(plan, seat, reverse, totals):
    total = jnp.zeros((plan.state_rows, HEAD_DIM), f32)
    for bit, other in zip(plan.bits, totals):
        upper = (seat & bit) != 0
        counts = jnp.logical_not(upper) if reverse else upper
        total = total + jnp.where(counts, other[plan.body, :], 0.0)
    return total


def state_at(plan, seat, reverse, x, outer, parts):
    here = seat % plan.group
    total = outer
    for y in range(plan.group):
        if y != x:
            ahead = (here ^ y) > (here ^ x) if reverse else (here ^ y) < (here ^ x)
            total = total + jnp.where(ahead, parts[y][plan.body, :], 0.0)
    return total


def state_kernel(plan, k_hbm, v_hbm, *refs):
    group = plan.group
    out, (k, v, sems) = refs[:group], refs[group:]
    seat = lax.axis_index("seq")
    pair = min(group, 2)
    copies = {}
    for x in range(0, group, pair):
        cols = plan.share(seat, x, pair)
        copies[x] = [
            pltpu.make_async_copy(src.at[:, cols], dst.at[:, cols], sems.at[i, x])
            for i, (src, dst) in enumerate(((k_hbm, k), (v_hbm, v)))
        ]
        for copy in copies[x]:
            copy.start()
    for x in range(group):
        for copy in copies.get(x, ()):
            copy.wait()
        for i in range(plan.own):
            cols = head_cols(plan.head_of(seat, x, i))
            out[x][rows_of(i), :] = dot(split(k[:, cols]), split(v[:, cols]), TN)


def local_kernel(plan, seat, q_hbm, k, v, target_hbm, gain, mask, q, flipped, scores, local, aim, count, target, sems):
    copies = [
        pltpu.make_async_copy(src, dst, sems.at[i]) for i, (src, dst) in enumerate(((q_hbm, q), (target_hbm, target)))
    ]
    for copy in copies:
        copy.start()
    causal = causal_mask(plan.length)
    valid = mask[...].astype(f32)
    count[...] = jnp.full((TAIL, HEAD_DIM), jnp.sum(valid), f32)
    valid = column(valid, plan.length)
    for copy in copies:
        copy.wait()
    for h in range(plan.heads):
        cols = head_cols(h)
        flipped[h] = q[:, cols].T
        s = dot(split(q[:, cols]), split(k[:, cols]), NT)
        s = jnp.where(causal, s, 0.0)
        scores[h] = s
        local[:, cols] = dot(split(s), split(v[:, cols]), NN)
        aim[:, cols] = valid * (gain[:, cols] * target[:, cols])


def total_kernel(plan, seat, *refs):
    parts, out = refs[:-1], refs[-1]
    out[plan.body, :] = pair_sum(r[plan.body, :] for r in parts)
    if out.shape[0] > plan.state_rows:
        out[plan.tail, :] = parts[0][plan.tail, :] + parts[plan.last][plan.tail, :]


def prior_kernel(plan, seat, *refs):
    group = plan.group
    parts, totals, outs = refs[:group], refs[group : -group], refs[-group:]
    outer = outer_sum(plan, seat[0], False, totals)
    for x in range(group):
        outs[x][...] = state_at(plan, seat[0], False, x, outer, parts)


def attend_kernel(plan, which, last, seat, q, local, aim, *refs):
    n = len(which)
    priors, refs = refs[:n], refs[n:]
    if last:
        squares, dots = refs[0][...], refs[1][...]
        refs = refs[2:]
    else:
        squares = jnp.zeros((plan.length, HEAD_DIM), f32)
        dots = jnp.zeros((plan.length, HEAD_DIM), f32)
    attended, sums = refs[:n], refs[n:]
    for x, prior, out in zip(which, priors, attended):
        for i in range(plan.own):
            cols = head_cols(plan.head_of(seat[0], x, i))
            a = local[:, cols] + dot(split(q[:, cols]), split(prior[rows_of(i), :]), NN)
            out[:, rows_of(i)] = a
            squares = squares + a * a
            dots = dots + aim[:, cols] * a
    if last:
        (stats,) = sums
        stats[0:1, :] = jnp.sum(squares.T, axis=0, keepdims=True)
        stats[1:2, :] = jnp.sum(dots.T, axis=0, keepdims=True)
        stats[2:, :] = jnp.zeros((TAIL - 2, plan.length), f32)
    else:
        sums[0][...] = squares
        sums[1][...] = dots


def scales(plan, stats):
    squares, dots = stats[0:1, :], stats[1:2, :]
    inverse_rms = lax.rsqrt(squares / plan.width + epsilon)
    loss = inverse_rms * dots
    return inverse_rms, inverse_rms * inverse_rms * loss / plan.width, loss


def grad_kernel(plan, seat, flipped, aim, count, *refs):
    refs = list(refs)
    take = lambda n: [refs.pop(0) for _ in range(n)]
    attended, stat_parts, (factors,), out = take(plan.group), take(plan.head), take(1), take(plan.group)
    left, right, losses = scales(plan, pair_sum(r[...] for r in stat_parts))
    factors[0:1, :] = left
    factors[1:2, :] = right
    left, right = column(left, plan.length), column(right, plan.length)
    row = lax.broadcasted_iota(jnp.int32, (TAIL, HEAD_DIM), 0)
    tail = jnp.where(row == 0, jnp.sum(losses), count[...])
    for x in range(plan.group):
        for i in range(plan.own):
            h = plan.head_of(seat[0], x, i)
            cols = head_cols(h)
            g = left * aim[:, cols] - right * attended[x][:, rows_of(i)]
            out[x][rows_of(i), :] = dot(split(flipped[h]), split(g), NN)
        if x in (0, plan.last):
            out[x][plan.tail, :] = tail


def local_grad_kernel(plan, seat, q, k, v, aim, factors, scores, *refs):
    group = plan.group
    attended, priors, (grad_q, grad_k, grad_v) = refs[:group], refs[group : 2 * group], refs[2 * group :]
    left, right = column(factors[0:1, :], plan.length), column(factors[1:2, :], plan.length)
    causal = causal_mask(plan.length)
    for x in range(plan.group):
        for i in range(plan.own):
            h = plan.head_of(seat[0], x, i)
            cols = head_cols(h)
            g = split(left * aim[:, cols] - right * attended[x][:, rows_of(i)])
            gs = split(jnp.where(causal, dot(g, split(v[:, cols]), NT), 0.0))
            prior = split(priors[x][rows_of(i), :])
            grad_q[:, cols] = dot(gs, split(k[:, cols]), NN) + dot(g, prior, NT)
            grad_k[:, cols] = dot(gs, split(q[:, cols]), TN)
            grad_v[:, cols] = dot(split(scores[h]), g, TN)


def later_kernel(plan, seat, *refs):
    group = plan.group
    states, totals, outs = refs[:group], refs[group : -group - 1], refs[-group:]
    outer = outer_sum(plan, seat[0], True, totals[1:])
    tail = totals[0][plan.tail, :]
    for other in totals[1:]:
        tail = tail + other[plan.tail, :]
    for x in range(group):
        outs[x][plan.body, :] = state_at(plan, seat[0], True, x, outer, states)
        if x == min(1, group - 1):
            outs[x][plan.tail, :] = tail


def final_kernel(plan, which, seat, k, v, part_k, part_v, sent, *refs):
    n = len(which)
    first = which[0] == 0
    later, refs = list(refs[:n]), refs[n:]
    if first:
        (part_q, loss, grad_q, grad_k, grad_v, block_k, block_v, block_q, sems) = refs
        tail = later[-1][plan.tail, :]
    else:
        (tail_ref, _, _, grad_k, grad_v, block_k, block_v, sems) = refs
        tail = tail_ref[plan.tail, :]
    if plan.group > 1:
        tail = sent[plan.tail, :] + tail
    factor = plan.tokens / tail[1:2, 0:1]
    copies = []
    for j, x in enumerate(which):
        for i in range(plan.own):
            cols = head_cols(plan.head_of(seat[0], x, i))
            state = split(later[j][rows_of(i), :])
            block_k[j, :, rows_of(i)] = factor * (part_k[:, cols] + dot(split(v[:, cols]), state, NT))
            block_v[j, :, rows_of(i)] = factor * (part_v[:, cols] + dot(split(k[:, cols]), state, NN))
        for m, (block, out) in enumerate(((block_k, grad_k), (block_v, grad_v))):
            copies.append(pltpu.make_async_copy(block.at[j], out.at[:, plan.share(seat[0], x)], sems.at[m, j]))
            copies[-1].start()
    if first:
        block_q[...] = factor * part_q[...]
        copies.append(pltpu.make_async_copy(block_q, grad_q, sems.at[2, 0]))
        copies[-1].start()
        loss[...] = tail[0:1, 0:1] / tail[1:2, 0:1]
    for copy in copies:
        copy.wait()


def swap(value, axis, step):
    return lax.ppermute(value, axis, [(i, i ^ step) for i in range(lax.axis_size(axis))])


def swap_all(parts, axis):
    return [parts[0]] + [swap(part, axis, x) for x, part in enumerate(parts) if x]


def swap_totals(plan, total):
    totals = [total]
    for step in plan.swaps:
        totals.append(swap(total, "seq", step))
        if step != plan.swaps[-1]:
            total = total + totals[-1]
    return totals


def shards(queries, key_rows, value_rows, target, norm_gain, valid_mask):
    length, columns = queries.shape
    heads = columns // HEAD_DIM
    head_count = lax.axis_size("head")
    plan = Plan(length, heads, lax.axis_size("seq"), head_count)
    group, own = plan.group, plan.own
    product = 6 * HEAD_DIM**3 * heads
    seat = jnp.reshape(lax.axis_index("seq"), (1,)).astype(jnp.int32)
    gain = norm_gain.reshape(1, columns)
    mask = valid_mask.reshape(1, length)
    sum_shape = shape(plan.state_rows + TAIL, HEAD_DIM)
    state = shape(plan.state_rows, HEAD_DIM)
    piece = shape(length, plan.state_rows)
    wide = shape(length, columns)
    bind = lambda kernel: functools.partial(kernel, plan)

    *kv, key_rows, value_rows = call(
        bind(state_kernel),
        [state] * group + [wide] * 2,
        product,
        None,
        in_hbm(key_rows),
        in_hbm(value_rows),
        specs=[ANY] * 2,
        scratch=[pltpu.SemaphoreType.DMA((2, group))],
    )
    queries, flipped, scores, local, aim, count = call(
        bind(local_kernel),
        [wide, shape(heads, HEAD_DIM, length), shape(heads, length, length), wide, wide, shape(TAIL, HEAD_DIM)],
        2 * product,
        seat,
        in_hbm(queries),
        key_rows,
        value_rows,
        in_hbm(target),
        in_hbm(gain),
        in_hbm(mask),
        specs=[ANY, VMEM, VMEM, ANY, VMEM, VMEM],
        scratch=[pltpu.VMEM((length, columns), f32), pltpu.SemaphoreType.DMA((2,))],
    )
    kv = swap_all(kv, "seq")
    (total,) = call(bind(total_kernel), [state], 0, seat, *kv)
    totals = swap_totals(plan, total)
    priors = call(bind(prior_kernel), [state] * group, 0, seat, *kv, *totals[1:])
    priors = swap_all(priors, "seq")
    early, late = list(range(group - 1)), [group - 1]
    column_sum = shape(length, HEAD_DIM)
    *attended, squares, dots = call(
        functools.partial(attend_kernel, plan, early, False),
        [piece] * len(early) + [column_sum] * 2,
        product,
        seat,
        queries,
        local,
        aim,
        *priors[:-1],
    )
    last, stats = call(
        functools.partial(attend_kernel, plan, late, True),
        [piece, shape(TAIL, length)],
        product // group,
        seat,
        queries,
        local,
        aim,
        priors[-1],
        squares,
        dots,
    )
    attended.append(last)
    stats = swap_all([stats] * head_count, "head")
    factors, *states = call(
        bind(grad_kernel),
        [shape(TAIL, length)] + [sum_shape if x in (0, plan.last) else state for x in range(group)],
        product,
        seat,
        flipped,
        aim,
        count,
        *attended,
        *stats,
    )
    part_query, part_key, part_value = call(
        bind(local_grad_kernel), [wide] * 3, 5 * product, seat, queries, key_rows, value_rows, aim, factors, scores, *attended, *priors
    )
    states = swap_all(states, "seq")
    (grad_total,) = call(bind(total_kernel), [sum_shape], 0, seat, *states)
    grad_totals = swap_totals(plan, grad_total)
    later = call(
        bind(later_kernel),
        [sum_shape if x == min(1, group - 1) else state for x in range(group)],
        0,
        seat,
        *states,
        *grad_totals,
        part_key,
        specs=[VMEM] * (group + len(grad_totals)) + [ANY],
    )
    sent = later[min(1, group - 1)]
    later = swap_all(later, "seq")
    grads = []
    for which in [early[:2], *([x] for x in early[2:]), late]:
        block = pltpu.VMEM((len(which), length, plan.state_rows), f32)
        inputs = [key_rows, value_rows, part_key, part_value, sent, *(later[x] for x in which)]
        if not grads:
            loss, grad_query, *grads = call(
                functools.partial(final_kernel, plan, which),
                [shape(1, 1), wide, wide, wide],
                2 * product * len(which) // group,
                seat,
                *inputs,
                part_query,
                out_specs=[VMEM] + [ANY] * 3,
                scratch=[block, block, pltpu.VMEM((length, columns), f32), pltpu.SemaphoreType.DMA((3, len(which)))],
            )
            continue
        inputs.append(later[1])
        grads = call(
            functools.partial(final_kernel, plan, which),
            [wide] * 2,
            2 * product * len(which) // group,
            seat,
            *inputs,
            *grads,
            specs=[VMEM] * len(inputs) + [ANY] * 2,
            out_specs=[ANY] * 2,
            scratch=[block, block, pltpu.SemaphoreType.DMA((2, len(which)))],
            aliases={1 + len(inputs) + i: i for i in range(2)},
        )
    grad_key, grad_value = grads
    return (grad_query, grad_key, grad_value, loss[0, 0])


def solution(mesh):
    return jax.shard_map(
        shards,
        mesh=mesh,
        in_specs=(
            P("seq", "head"),
            P("seq", "head"),
            P("seq", "head"),
            P("seq", "head"),
            P("head"),
            P("seq"),
        ),
        out_specs=(P("seq", "head"), P("seq", "head"), P("seq", "head"), P()),
        check_vma=False,
    )
```

```python
import functools

import jax
import jax.numpy as jnp
from jax import lax
from jax.experimental import pallas as pl
from jax.experimental.pallas import tpu as pltpu
from jax.sharding import PartitionSpec as P

HEAD_DIM = 128
TAIL = 8
epsilon = 1e-06
f32 = jnp.float32
bf16 = jnp.bfloat16
SMEM = pl.BlockSpec(memory_space=pltpu.SMEM)
VMEM = pl.BlockSpec(memory_space=pltpu.VMEM)
ANY = pl.BlockSpec(memory_space=pl.ANY)

NN = ((1,), (0,))
NT = ((1,), (1,))
TN = ((0,), (0,))


def split(x):
    high = x.astype(bf16)
    return high, (x - high.astype(f32)).astype(bf16)


def dot(a, b, dims):
    ca, cb = dims[0][0], dims[1][0]
    left = jnp.concatenate(a, axis=ca)
    both = jnp.concatenate(b, axis=1 - cb)
    right = jnp.concatenate([both, both], axis=cb)
    out = lax.dot_general(left, right, (dims, ((), ())), preferred_element_type=f32)
    n = out.shape[1] // 2
    return out[:, :n] + out[:, n:]


def head_cols(h):
    return pl.ds(pl.multiple_of(h * HEAD_DIM, HEAD_DIM), HEAD_DIM)


def rows_of(i):
    return slice(i * HEAD_DIM, (i + 1) * HEAD_DIM)


def in_hbm(x):
    return pltpu.with_memory_space_constraint(x, pltpu.HBM)


def shape(*s):
    return jax.ShapeDtypeStruct(s, f32)


def call(kernel, outs, flops, seat, *args, specs=None, out_specs=None, scratch=(), aliases=None, limit=24):
    specs = specs or [VMEM] * len(args)
    place = [] if seat is None else [seat]
    nbytes = sum(a.size * 4 for a in args) + sum(o.size * 4 for o in outs)
    return pl.pallas_call(
        kernel,
        out_shape=outs,
        in_specs=[SMEM] * len(place) + specs,
        out_specs=out_specs or [VMEM] * len(outs),
        scratch_shapes=scratch,
        input_output_aliases=aliases or {},
        compiler_params=pltpu.CompilerParams(vmem_limit_bytes=limit * 1024 * 1024),
        cost_estimate=pl.CostEstimate(flops=flops, bytes_accessed=nbytes, transcendentals=0),
    )(*place, *args)


def causal_mask(n):
    return lax.broadcasted_iota(jnp.int32, (n, n), 0) >= lax.broadcasted_iota(jnp.int32, (n, n), 1)


def column(row, n):
    return jnp.broadcast_to(row, (HEAD_DIM, n)).T


def pair_sum(parts):
    parts = list(parts)
    while len(parts) > 1:
        parts = [parts[i] + parts[i + 1] for i in range(0, len(parts), 2)]
    return parts[0]


class Plan:
    def __init__(self, length, heads, seq, head):
        group = 1
        while group < 4 and seq % (2 * group) == 0 and heads % (2 * group) == 0:
            group *= 2
        self.length, self.heads, self.head, self.group, self.own = length, heads, head, group, heads // group
        self.width, self.tokens = heads * HEAD_DIM * head, length * seq
        self.bits = [group << i for i in range(30) if group << i < seq]
        self.swaps = [bit | (bit // 2 if bit == group else 0) for bit in self.bits]
        self.state_rows = self.own * HEAD_DIM
        self.last = group // 2
        self.body = slice(0, self.state_rows)
        self.tail = slice(self.state_rows, self.state_rows + TAIL)

    def owned(self, seat, x):
        return (seat % self.group) ^ ((seat & self.group) // 2) ^ x

    def head_of(self, seat, x, i):
        return self.owned(seat, x) * self.own + i

    def share(self, seat, x, count=1):
        start = self.owned(seat, x) // count * (count * self.state_rows)
        return pl.ds(pl.multiple_of(start, HEAD_DIM), count * self.state_rows)


def outer_sum(plan, seat, reverse, totals):
    total = jnp.zeros((plan.state_rows, HEAD_DIM), f32)
    for bit, other in zip(plan.bits, totals):
        upper = (seat & bit) != 0
        counts = jnp.logical_not(upper) if reverse else upper
        total = total + jnp.where(counts, other[plan.body, :], 0.0)
    return total


def state_at(plan, seat, reverse, x, outer, parts):
    here = seat % plan.group
    total = outer
    for y in range(plan.group):
        if y != x:
            ahead = (here ^ y) > (here ^ x) if reverse else (here ^ y) < (here ^ x)
            total = total + jnp.where(ahead, parts[y][plan.body, :], 0.0)
    return total


def state_kernel(plan, k_hbm, v_hbm, *refs):
    group = plan.group
    out, (k, v, sems) = refs[:group], refs[group:]
    seat = lax.axis_index("seq")
    pair = min(group, 2)
    copies = {}
    for x in range(0, group, pair):
        cols = plan.share(seat, x, pair)
        copies[x] = [
            pltpu.make_async_copy(src.at[:, cols], dst.at[:, cols], sems.at[i, x])
            for i, (src, dst) in enumerate(((k_hbm, k), (v_hbm, v)))
        ]
        for copy in copies[x]:
            copy.start()
    for x in range(group):
        for copy in copies.get(x, ()):
            copy.wait()
        for i in range(plan.own):
            cols = head_cols(plan.head_of(seat, x, i))
            out[x][rows_of(i), :] = dot(split(k[:, cols]), split(v[:, cols]), TN)


def local_kernel(plan, seat, q_hbm, k, v, target_hbm, gain, mask, q, flipped, scores, local, aim, count, target, sems):
    copies = [
        pltpu.make_async_copy(src, dst, sems.at[i]) for i, (src, dst) in enumerate(((q_hbm, q), (target_hbm, target)))
    ]
    for copy in copies:
        copy.start()
    causal = causal_mask(plan.length)
    valid = mask[...].astype(f32)
    count[...] = jnp.full((TAIL, HEAD_DIM), jnp.sum(valid), f32)
    valid = column(valid, plan.length)
    for copy in copies:
        copy.wait()
    for h in range(plan.heads):
        cols = head_cols(h)
        flipped[h] = q[:, cols].T
        s = dot(split(q[:, cols]), split(k[:, cols]), NT)
        s = jnp.where(causal, s, 0.0)
        scores[h] = s
        local[:, cols] = dot(split(s), split(v[:, cols]), NN)
        aim[:, cols] = valid * (gain[:, cols] * target[:, cols])


def total_kernel(plan, seat, *refs):
    parts, out = refs[:-1], refs[-1]
    out[plan.body, :] = pair_sum(r[plan.body, :] for r in parts)
    if out.shape[0] > plan.state_rows:
        out[plan.tail, :] = parts[0][plan.tail, :] + parts[plan.last][plan.tail, :]


def prior_kernel(plan, seat, *refs):
    group = plan.group
    parts, totals, outs = refs[:group], refs[group : -group - 1], refs[-group:]
    outer = outer_sum(plan, seat[0], False, totals)
    for x in range(group):
        outs[x][...] = state_at(plan, seat[0], False, x, outer, parts)


def attend_kernel(plan, which, last, seat, q, local, aim, *refs):
    n = len(which)
    priors, refs = refs[:n], refs[n:]
    if last:
        squares, dots = refs[0][...], refs[1][...]
        refs = refs[2:]
    else:
        squares = jnp.zeros((plan.length, HEAD_DIM), f32)
        dots = jnp.zeros((plan.length, HEAD_DIM), f32)
    attended, sums = refs[:n], refs[n:]
    for x, prior, out in zip(which, priors, attended):
        for i in range(plan.own):
            cols = head_cols(plan.head_of(seat[0], x, i))
            a = local[:, cols] + dot(split(q[:, cols]), split(prior[rows_of(i), :]), NN)
            out[:, rows_of(i)] = a
            squares = squares + a * a
            dots = dots + aim[:, cols] * a
    if last:
        (stats,) = sums
        stats[0:1, :] = jnp.sum(squares.T, axis=0, keepdims=True)
        stats[1:2, :] = jnp.sum(dots.T, axis=0, keepdims=True)
        stats[2:, :] = jnp.zeros((TAIL - 2, plan.length), f32)
    else:
        sums[0][...] = squares
        sums[1][...] = dots


def scales(plan, stats):
    squares, dots = stats[0:1, :], stats[1:2, :]
    inverse_rms = lax.rsqrt(squares / plan.width + epsilon)
    loss = inverse_rms * dots
    return inverse_rms, inverse_rms * inverse_rms * loss / plan.width, loss


def grad_kernel(plan, seat, flipped, aim, count, *refs):
    refs = list(refs)
    take = lambda n: [refs.pop(0) for _ in range(n)]
    attended, stat_parts, (factors,), out = take(plan.group), take(plan.head), take(1), take(plan.group)
    left, right, losses = scales(plan, pair_sum(r[...] for r in stat_parts))
    factors[0:1, :] = left
    factors[1:2, :] = right
    left, right = column(left, plan.length), column(right, plan.length)
    row = lax.broadcasted_iota(jnp.int32, (TAIL, HEAD_DIM), 0)
    tail = jnp.where(row == 0, jnp.sum(losses), count[...])
    for x in range(plan.group):
        for i in range(plan.own):
            h = plan.head_of(seat[0], x, i)
            cols = head_cols(h)
            g = left * aim[:, cols] - right * attended[x][:, rows_of(i)]
            out[x][rows_of(i), :] = dot(split(flipped[h]), split(g), NN)
        if x in (0, plan.last):
            out[x][plan.tail, :] = tail


def local_grad_kernel(plan, seat, q, k, v, aim, factors, scores, *refs):
    group = plan.group
    attended, priors, (grad_q, grad_k, grad_v) = refs[:group], refs[group : 2 * group], refs[2 * group :]
    left, right = column(factors[0:1, :], plan.length), column(factors[1:2, :], plan.length)
    causal = causal_mask(plan.length)
    for x in range(plan.group):
        for i in range(plan.own):
            h = plan.head_of(seat[0], x, i)
            cols = head_cols(h)
            g = split(left * aim[:, cols] - right * attended[x][:, rows_of(i)])
            gs = split(jnp.where(causal, dot(g, split(v[:, cols]), NT), 0.0))
            prior = split(priors[x][rows_of(i), :])
            grad_q[:, cols] = dot(gs, split(k[:, cols]), NN) + dot(g, prior, NT)
            grad_k[:, cols] = dot(gs, split(q[:, cols]), TN)
            grad_v[:, cols] = dot(split(scores[h]), g, TN)


def later_kernel(plan, seat, *refs):
    group = plan.group
    states, totals, outs = refs[:group], refs[group : -group - 1], refs[-group:]
    outer = outer_sum(plan, seat[0], True, totals[1:])
    tail = totals[0][plan.tail, :]
    for other in totals[1:]:
        tail = tail + other[plan.tail, :]
    for x in range(group):
        outs[x][plan.body, :] = state_at(plan, seat[0], True, x, outer, states)
        if x == min(1, group - 1):
            outs[x][plan.tail, :] = tail


def final_kernel(plan, which, seat, k, v, part_k, part_v, sent, *refs):
    n = len(which)
    first = which[0] == 0
    later, refs = list(refs[:n]), refs[n:]
    if first:
        (part_q, loss, grad_q, grad_k, grad_v, block_k, block_v, block_q, sems) = refs
        tail = later[-1][plan.tail, :]
    else:
        (tail_ref, _, _, grad_k, grad_v, block_k, block_v, sems) = refs
        tail = tail_ref[plan.tail, :]
    if plan.group > 1:
        tail = sent[plan.tail, :] + tail
    factor = plan.tokens / tail[1:2, 0:1]
    copies = []
    for j, x in enumerate(which):
        for i in range(plan.own):
            cols = head_cols(plan.head_of(seat[0], x, i))
            state = split(later[j][rows_of(i), :])
            block_k[j, :, rows_of(i)] = factor * (part_k[:, cols] + dot(split(v[:, cols]), state, NT))
            block_v[j, :, rows_of(i)] = factor * (part_v[:, cols] + dot(split(k[:, cols]), state, NN))
            for m, (block, out) in enumerate(((block_k, grad_k), (block_v, grad_v))):
                copies.append(
                    pltpu.make_async_copy(block.at[j, :, rows_of(i)], out.at[:, cols], sems.at[m, j * plan.own + i])
                )
                copies[-1].start()
    if first:
        block_q[...] = factor * part_q[...]
        copies.append(pltpu.make_async_copy(block_q, grad_q, sems.at[2, 0]))
        copies[-1].start()
        loss[...] = tail[0:1, 0:1] / tail[1:2, 0:1]
    for copy in copies:
        copy.wait()


def swap(value, axis, step):
    return lax.ppermute(value, axis, [(i, i ^ step) for i in range(lax.axis_size(axis))])


def swap_all(parts, axis):
    return [parts[0]] + [swap(part, axis, x) for x, part in enumerate(parts) if x]


def swap_totals(plan, total):
    totals = [total]
    for step in plan.swaps:
        totals.append(swap(total, "seq", step))
        if step != plan.swaps[-1]:
            total = total + totals[-1]
    return totals


def shards(queries, key_rows, value_rows, target, norm_gain, valid_mask):
    length, columns = queries.shape
    heads = columns // HEAD_DIM
    head_count = lax.axis_size("head")
    plan = Plan(length, heads, lax.axis_size("seq"), head_count)
    group, own = plan.group, plan.own
    product = 6 * HEAD_DIM**3 * heads
    seat = jnp.reshape(lax.axis_index("seq"), (1,)).astype(jnp.int32)
    gain = norm_gain.reshape(1, columns)
    mask = valid_mask.reshape(1, length)
    sum_shape = shape(plan.state_rows + TAIL, HEAD_DIM)
    state = shape(plan.state_rows, HEAD_DIM)
    piece = shape(length, plan.state_rows)
    wide = shape(length, columns)
    bind = lambda kernel: functools.partial(kernel, plan)

    *kv, key_rows, value_rows = call(
        bind(state_kernel),
        [state] * group + [wide] * 2,
        product,
        None,
        in_hbm(key_rows),
        in_hbm(value_rows),
        specs=[ANY] * 2,
        scratch=[pltpu.SemaphoreType.DMA((2, group))],
    )
    queries, flipped, scores, local, aim, count = call(
        bind(local_kernel),
        [wide, shape(heads, HEAD_DIM, length), shape(heads, length, length), wide, wide, shape(TAIL, HEAD_DIM)],
        2 * product,
        seat,
        in_hbm(queries),
        key_rows,
        value_rows,
        in_hbm(target),
        in_hbm(gain),
        in_hbm(mask),
        specs=[ANY, VMEM, VMEM, ANY, VMEM, VMEM],
        scratch=[pltpu.VMEM((length, columns), f32), pltpu.SemaphoreType.DMA((2,))],
    )
    kv = swap_all(kv, "seq")
    (total,) = call(bind(total_kernel), [state], 0, seat, *kv)
    totals = swap_totals(plan, total)
    priors = call(
        bind(prior_kernel),
        [state] * group,
        0,
        seat,
        *kv,
        *totals[1:],
        scores,
        specs=[VMEM] * (group + len(totals) - 1) + [ANY],
    )
    priors = swap_all(priors, "seq")
    early, late = list(range(group - 1)), [group - 1]
    column_sum = shape(length, HEAD_DIM)
    *attended, squares, dots = call(
        functools.partial(attend_kernel, plan, early, False),
        [piece] * len(early) + [column_sum] * 2,
        product,
        seat,
        queries,
        local,
        aim,
        *priors[:-1],
    )
    last, stats = call(
        functools.partial(attend_kernel, plan, late, True),
        [piece, shape(TAIL, length)],
        product // group,
        seat,
        queries,
        local,
        aim,
        priors[-1],
        squares,
        dots,
    )
    attended.append(last)
    stats = swap_all([stats] * head_count, "head")
    factors, *states = call(
        bind(grad_kernel),
        [shape(TAIL, length)] + [sum_shape if x in (0, plan.last) else state for x in range(group)],
        product,
        seat,
        flipped,
        aim,
        count,
        *attended,
        *stats,
    )
    part_query, part_key, part_value = call(
        bind(local_grad_kernel), [wide] * 3, 5 * product, seat, queries, key_rows, value_rows, aim, factors, scores, *attended, *priors
    )
    states = swap_all(states, "seq")
    (grad_total,) = call(bind(total_kernel), [sum_shape], 0, seat, *states)
    grad_totals = swap_totals(plan, grad_total)
    later = call(
        bind(later_kernel),
        [sum_shape if x == min(1, group - 1) else state for x in range(group)],
        0,
        seat,
        *states,
        *grad_totals,
        part_key,
        specs=[VMEM] * (group + len(grad_totals)) + [ANY],
    )
    sent = later[min(1, group - 1)]
    later = swap_all(later, "seq")
    grads = []
    for which in [early[:2], *([x] for x in early[2:]), late]:
        block = pltpu.VMEM((len(which), length, plan.state_rows), f32)
        inputs = [key_rows, value_rows, part_key, part_value, sent, *(later[x] for x in which)]
        if not grads:
            loss, grad_query, *grads = call(
                functools.partial(final_kernel, plan, which),
                [shape(1, 1), wide, wide, wide],
                2 * product * len(which) // group,
                seat,
                *inputs,
                part_query,
                out_specs=[VMEM] + [ANY] * 3,
                scratch=[block, block, pltpu.VMEM((length, columns), f32), pltpu.SemaphoreType.DMA((3, own * len(which)))],
            )
            continue
        inputs.append(later[1])
        grads = call(
            functools.partial(final_kernel, plan, which),
            [wide] * 2,
            2 * product * len(which) // group,
            seat,
            *inputs,
            *grads,
            specs=[VMEM] * len(inputs) + [ANY] * 2,
            out_specs=[ANY] * 2,
            scratch=[block, block, pltpu.SemaphoreType.DMA((2, own * len(which)))],
            aliases={1 + len(inputs) + i: i for i in range(2)},
        )
    grad_key, grad_value = grads
    return (grad_query, grad_key, grad_value, loss[0, 0])


def solution(mesh):
    return jax.shard_map(
        shards,
        mesh=mesh,
        in_specs=(
            P("seq", "head"),
            P("seq", "head"),
            P("seq", "head"),
            P("seq", "head"),
            P("head"),
            P("seq"),
        ),
        out_specs=(P("seq", "head"), P("seq", "head"), P("seq", "head"), P()),
        check_vma=False,
    )
```

```python
import functools

import jax
import jax.numpy as jnp
from jax import lax
from jax.experimental import pallas as pl
from jax.experimental.pallas import tpu as pltpu
from jax.sharding import PartitionSpec as P

HEAD_DIM = 128
TAIL = 8
epsilon = 1e-06
f32 = jnp.float32
bf16 = jnp.bfloat16
SMEM = pl.BlockSpec(memory_space=pltpu.SMEM)
VMEM = pl.BlockSpec(memory_space=pltpu.VMEM)
ANY = pl.BlockSpec(memory_space=pl.ANY)

NN = ((1,), (0,))
NT = ((1,), (1,))
TN = ((0,), (0,))


def split(x):
    high = x.astype(bf16)
    return high, (x - high.astype(f32)).astype(bf16)


def dot(a, b, dims):
    ca, cb = dims[0][0], dims[1][0]
    left = jnp.concatenate(a, axis=ca)
    both = jnp.concatenate(b, axis=1 - cb)
    right = jnp.concatenate([both, both], axis=cb)
    out = lax.dot_general(left, right, (dims, ((), ())), preferred_element_type=f32)
    n = out.shape[1] // 2
    return out[:, :n] + out[:, n:]


def head_cols(h):
    return pl.ds(pl.multiple_of(h * HEAD_DIM, HEAD_DIM), HEAD_DIM)


def rows_of(i):
    return slice(i * HEAD_DIM, (i + 1) * HEAD_DIM)


def in_hbm(x):
    return pltpu.with_memory_space_constraint(x, pltpu.HBM)


def shape(*s):
    return jax.ShapeDtypeStruct(s, f32)


def call(kernel, outs, flops, seat, *args, specs=None, out_specs=None, scratch=(), aliases=None, limit=24):
    specs = specs or [VMEM] * len(args)
    place = [] if seat is None else [seat]
    nbytes = sum(a.size * 4 for a in args) + sum(o.size * 4 for o in outs)
    return pl.pallas_call(
        kernel,
        out_shape=outs,
        in_specs=[SMEM] * len(place) + specs,
        out_specs=out_specs or [VMEM] * len(outs),
        scratch_shapes=scratch,
        input_output_aliases=aliases or {},
        compiler_params=pltpu.CompilerParams(vmem_limit_bytes=limit * 1024 * 1024),
        cost_estimate=pl.CostEstimate(flops=flops, bytes_accessed=nbytes, transcendentals=0),
    )(*place, *args)


def causal_mask(n):
    return lax.broadcasted_iota(jnp.int32, (n, n), 0) >= lax.broadcasted_iota(jnp.int32, (n, n), 1)


def column(row, n):
    return jnp.broadcast_to(row, (HEAD_DIM, n)).T


def pair_sum(parts):
    parts = list(parts)
    while len(parts) > 1:
        parts = [parts[i] + parts[i + 1] for i in range(0, len(parts), 2)]
    return parts[0]


class Plan:
    def __init__(self, length, heads, seq, head):
        group = 1
        while group < 4 and seq % (2 * group) == 0 and heads % (2 * group) == 0:
            group *= 2
        self.length, self.heads, self.head, self.group, self.own = length, heads, head, group, heads // group
        self.width, self.tokens = heads * HEAD_DIM * head, length * seq
        self.bits = [group << i for i in range(30) if group << i < seq]
        self.swaps = [bit | (bit // 2 if bit == group else 0) for bit in self.bits]
        self.state_rows = self.own * HEAD_DIM
        self.last = group // 2
        self.body = slice(0, self.state_rows)
        self.tail = slice(self.state_rows, self.state_rows + TAIL)

    def owned(self, seat, x):
        return (seat % self.group) ^ ((seat & self.group) // 2) ^ x

    def head_of(self, seat, x, i):
        return self.owned(seat, x) * self.own + i

    def share(self, seat, x, count=1):
        start = self.owned(seat, x) // count * (count * self.state_rows)
        return pl.ds(pl.multiple_of(start, HEAD_DIM), count * self.state_rows)


def outer_sum(plan, seat, reverse, totals):
    total = jnp.zeros((plan.state_rows, HEAD_DIM), f32)
    for bit, other in zip(plan.bits, totals):
        upper = (seat & bit) != 0
        counts = jnp.logical_not(upper) if reverse else upper
        total = total + jnp.where(counts, other[plan.body, :], 0.0)
    return total


def state_at(plan, seat, reverse, x, outer, parts):
    here = seat % plan.group
    total = outer
    for y in range(plan.group):
        if y != x:
            ahead = (here ^ y) > (here ^ x) if reverse else (here ^ y) < (here ^ x)
            total = total + jnp.where(ahead, parts[y][plan.body, :], 0.0)
    return total


def state_kernel(plan, k_hbm, v_hbm, *refs):
    group = plan.group
    out, (k, v, sems) = refs[:group], refs[group:]
    seat = lax.axis_index("seq")
    pair = min(group, 2)
    copies = {}
    for x in range(0, group, pair):
        cols = plan.share(seat, x, pair)
        copies[x] = [
            pltpu.make_async_copy(src.at[:, cols], dst.at[:, cols], sems.at[i, x])
            for i, (src, dst) in enumerate(((k_hbm, k), (v_hbm, v)))
        ]
        for copy in copies[x]:
            copy.start()
    for x in range(group):
        for copy in copies.get(x, ()):
            copy.wait()
        for i in range(plan.own):
            cols = head_cols(plan.head_of(seat, x, i))
            out[x][rows_of(i), :] = dot(split(k[:, cols]), split(v[:, cols]), TN)


def local_kernel(plan, seat, q_hbm, k, v, target_hbm, gain, mask, q, flipped, scores, local, aim, count, target, sems):
    copies = [
        pltpu.make_async_copy(src, dst, sems.at[i]) for i, (src, dst) in enumerate(((q_hbm, q), (target_hbm, target)))
    ]
    for copy in copies:
        copy.start()
    causal = causal_mask(plan.length)
    valid = mask[...].astype(f32)
    count[...] = jnp.full((TAIL, HEAD_DIM), jnp.sum(valid), f32)
    valid = column(valid, plan.length)
    for copy in copies:
        copy.wait()
    for h in range(plan.heads):
        cols = head_cols(h)
        flipped[h] = q[:, cols].T
        s = dot(split(q[:, cols]), split(k[:, cols]), NT)
        s = jnp.where(causal, s, 0.0)
        scores[h] = s
        local[:, cols] = dot(split(s), split(v[:, cols]), NN)
        aim[:, cols] = valid * (gain[:, cols] * target[:, cols])


def total_kernel(plan, seat, *refs):
    parts, out = refs[:-1], refs[-1]
    out[plan.body, :] = pair_sum(r[plan.body, :] for r in parts)
    if out.shape[0] > plan.state_rows:
        out[plan.tail, :] = parts[0][plan.tail, :] + parts[plan.last][plan.tail, :]


def prior_kernel(plan, seat, *refs):
    group = plan.group
    parts, totals, outs = refs[:group], refs[group : -group - 1], refs[-group:]
    outer = outer_sum(plan, seat[0], False, totals)
    for x in range(group):
        outs[x][...] = state_at(plan, seat[0], False, x, outer, parts)


def attend_kernel(plan, which, last, seat, q, local, aim, *refs):
    n = len(which)
    priors, refs = refs[:n], refs[n:]
    if last:
        squares, dots = refs[0][...], refs[1][...]
        refs = refs[2:]
    else:
        squares = jnp.zeros((plan.length, HEAD_DIM), f32)
        dots = jnp.zeros((plan.length, HEAD_DIM), f32)
    attended, sums = refs[:n], refs[n:]
    for x, prior, out in zip(which, priors, attended):
        for i in range(plan.own):
            cols = head_cols(plan.head_of(seat[0], x, i))
            a = local[:, cols] + dot(split(q[:, cols]), split(prior[rows_of(i), :]), NN)
            out[:, rows_of(i)] = a
            squares = squares + a * a
            dots = dots + aim[:, cols] * a
    if last:
        (stats,) = sums
        stats[0:1, :] = jnp.sum(squares.T, axis=0, keepdims=True)
        stats[1:2, :] = jnp.sum(dots.T, axis=0, keepdims=True)
        stats[2:, :] = jnp.zeros((TAIL - 2, plan.length), f32)
    else:
        sums[0][...] = squares
        sums[1][...] = dots


def scales(plan, stats):
    squares, dots = stats[0:1, :], stats[1:2, :]
    inverse_rms = lax.rsqrt(squares / plan.width + epsilon)
    loss = inverse_rms * dots
    return inverse_rms, inverse_rms * inverse_rms * loss / plan.width, loss


def grad_kernel(plan, seat, flipped, aim, count, *refs):
    refs = list(refs)
    take = lambda n: [refs.pop(0) for _ in range(n)]
    attended, stat_parts, (factors,), out = take(plan.group), take(plan.head), take(1), take(plan.group)
    left, right, losses = scales(plan, pair_sum(r[...] for r in stat_parts))
    factors[0:1, :] = left
    factors[1:2, :] = right
    left, right = column(left, plan.length), column(right, plan.length)
    row = lax.broadcasted_iota(jnp.int32, (TAIL, HEAD_DIM), 0)
    tail = jnp.where(row == 0, jnp.sum(losses), count[...])
    for x in range(plan.group):
        for i in range(plan.own):
            h = plan.head_of(seat[0], x, i)
            cols = head_cols(h)
            g = left * aim[:, cols] - right * attended[x][:, rows_of(i)]
            out[x][rows_of(i), :] = dot(split(flipped[h]), split(g), NN)
        if x in (0, plan.last):
            out[x][plan.tail, :] = tail


def local_grad_kernel(plan, seat, q, k, v, aim, factors, scores, *refs):
    group = plan.group
    attended, priors, (grad_q, grad_k, grad_v) = refs[:group], refs[group : 2 * group], refs[2 * group :]
    left, right = column(factors[0:1, :], plan.length), column(factors[1:2, :], plan.length)
    causal = causal_mask(plan.length)
    for x in range(plan.group):
        for i in range(plan.own):
            h = plan.head_of(seat[0], x, i)
            cols = head_cols(h)
            g = split(left * aim[:, cols] - right * attended[x][:, rows_of(i)])
            gs = split(jnp.where(causal, dot(g, split(v[:, cols]), NT), 0.0))
            prior = split(priors[x][rows_of(i), :])
            grad_q[:, cols] = dot(gs, split(k[:, cols]), NN) + dot(g, prior, NT)
            grad_k[:, cols] = dot(gs, split(q[:, cols]), TN)
            grad_v[:, cols] = dot(split(scores[h]), g, TN)


def later_kernel(plan, seat, *refs):
    group = plan.group
    states, totals, outs = refs[:group], refs[group:-group], refs[-group:]
    outer = outer_sum(plan, seat[0], True, totals[1:])
    tail = totals[0][plan.tail, :]
    for other in totals[1:]:
        tail = tail + other[plan.tail, :]
    for x in range(group):
        outs[x][plan.body, :] = state_at(plan, seat[0], True, x, outer, states)
        if x == min(1, group - 1):
            outs[x][plan.tail, :] = tail


def final_kernel(plan, which, seat, k, v, part_k, part_v, sent, *refs):
    n = len(which)
    first = which[0] == 0
    later, refs = list(refs[:n]), refs[n:]
    if first:
        (part_q, loss, grad_q, grad_k, grad_v, block_k, block_v, block_q, sems) = refs
        tail = later[-1][plan.tail, :]
    else:
        (tail_ref, _, _, grad_k, grad_v, block_k, block_v, sems) = refs
        tail = tail_ref[plan.tail, :]
    if plan.group > 1:
        tail = sent[plan.tail, :] + tail
    factor = plan.tokens / tail[1:2, 0:1]
    copies = []
    for j, x in enumerate(which):
        for i in range(plan.own):
            cols = head_cols(plan.head_of(seat[0], x, i))
            state = split(later[j][rows_of(i), :])
            block_k[j, :, rows_of(i)] = factor * (part_k[:, cols] + dot(split(v[:, cols]), state, NT))
            block_v[j, :, rows_of(i)] = factor * (part_v[:, cols] + dot(split(k[:, cols]), state, NN))
            for m, (block, out) in enumerate(((block_k, grad_k), (block_v, grad_v))):
                copies.append(
                    pltpu.make_async_copy(block.at[j, :, rows_of(i)], out.at[:, cols], sems.at[m, j * plan.own + i])
                )
                copies[-1].start()
    if first:
        block_q[...] = factor * part_q[...]
        copies.append(pltpu.make_async_copy(block_q, grad_q, sems.at[2, 0]))
        copies[-1].start()
        loss[...] = tail[0:1, 0:1] / tail[1:2, 0:1]
    for copy in copies:
        copy.wait()


def swap(value, axis, step):
    return lax.ppermute(value, axis, [(i, i ^ step) for i in range(lax.axis_size(axis))])


def swap_all(parts, axis):
    return [parts[0]] + [swap(part, axis, x) for x, part in enumerate(parts) if x]


def swap_totals(plan, total):
    totals = [total]
    for step in plan.swaps:
        totals.append(swap(total, "seq", step))
        if step != plan.swaps[-1]:
            total = total + totals[-1]
    return totals


def shards(queries, key_rows, value_rows, target, norm_gain, valid_mask):
    length, columns = queries.shape
    heads = columns // HEAD_DIM
    head_count = lax.axis_size("head")
    plan = Plan(length, heads, lax.axis_size("seq"), head_count)
    group, own = plan.group, plan.own
    product = 6 * HEAD_DIM**3 * heads
    seat = jnp.reshape(lax.axis_index("seq"), (1,)).astype(jnp.int32)
    gain = norm_gain.reshape(1, columns)
    mask = valid_mask.reshape(1, length)
    sum_shape = shape(plan.state_rows + TAIL, HEAD_DIM)
    state = shape(plan.state_rows, HEAD_DIM)
    piece = shape(length, plan.state_rows)
    wide = shape(length, columns)
    bind = lambda kernel: functools.partial(kernel, plan)

    *kv, key_rows, value_rows = call(
        bind(state_kernel),
        [state] * group + [wide] * 2,
        product,
        None,
        in_hbm(key_rows),
        in_hbm(value_rows),
        specs=[ANY] * 2,
        scratch=[pltpu.SemaphoreType.DMA((2, group))],
    )
    queries, flipped, scores, local, aim, count = call(
        bind(local_kernel),
        [wide, shape(heads, HEAD_DIM, length), shape(heads, length, length), wide, wide, shape(TAIL, HEAD_DIM)],
        2 * product,
        seat,
        in_hbm(queries),
        key_rows,
        value_rows,
        in_hbm(target),
        in_hbm(gain),
        in_hbm(mask),
        specs=[ANY, VMEM, VMEM, ANY, VMEM, VMEM],
        scratch=[pltpu.VMEM((length, columns), f32), pltpu.SemaphoreType.DMA((2,))],
    )
    kv = swap_all(kv, "seq")
    (total,) = call(bind(total_kernel), [state], 0, seat, *kv)
    totals = swap_totals(plan, total)
    priors = call(
        bind(prior_kernel),
        [state] * group,
        0,
        seat,
        *kv,
        *totals[1:],
        scores,
        specs=[VMEM] * (group + len(totals) - 1) + [ANY],
    )
    priors = swap_all(priors, "seq")
    early, late = list(range(group - 1)), [group - 1]
    column_sum = shape(length, HEAD_DIM)
    *attended, squares, dots = call(
        functools.partial(attend_kernel, plan, early, False),
        [piece] * len(early) + [column_sum] * 2,
        product,
        seat,
        queries,
        local,
        aim,
        *priors[:-1],
    )
    last, stats = call(
        functools.partial(attend_kernel, plan, late, True),
        [piece, shape(TAIL, length)],
        product // group,
        seat,
        queries,
        local,
        aim,
        priors[-1],
        squares,
        dots,
    )
    attended.append(last)
    stats = swap_all([stats] * head_count, "head")
    factors, *states = call(
        bind(grad_kernel),
        [shape(TAIL, length)] + [sum_shape if x in (0, plan.last) else state for x in range(group)],
        product,
        seat,
        flipped,
        aim,
        count,
        *attended,
        *stats,
    )
    part_query, part_key, part_value = call(
        bind(local_grad_kernel), [wide] * 3, 5 * product, seat, queries, key_rows, value_rows, aim, factors, scores, *attended, *priors
    )
    states = swap_all(states, "seq")
    (grad_total,) = call(bind(total_kernel), [sum_shape], 0, seat, *states)
    grad_totals = swap_totals(plan, grad_total)
    later = call(
        bind(later_kernel),
        [sum_shape if x == min(1, group - 1) else state for x in range(group)],
        0,
        seat,
        *states,
        *grad_totals,
    )
    sent = later[min(1, group - 1)]
    later = swap_all(later, "seq")
    grads = []
    for which in [early[:2], *([x] for x in early[2:]), late]:
        block = pltpu.VMEM((len(which), length, plan.state_rows), f32)
        inputs = [key_rows, value_rows, part_key, part_value, sent, *(later[x] for x in which)]
        if not grads:
            loss, grad_query, *grads = call(
                functools.partial(final_kernel, plan, which),
                [shape(1, 1), wide, wide, wide],
                2 * product * len(which) // group,
                seat,
                *inputs,
                part_query,
                out_specs=[VMEM] + [ANY] * 3,
                scratch=[block, block, pltpu.VMEM((length, columns), f32), pltpu.SemaphoreType.DMA((3, own * len(which)))],
            )
            continue
        inputs.append(later[1])
        grads = call(
            functools.partial(final_kernel, plan, which),
            [wide] * 2,
            2 * product * len(which) // group,
            seat,
            *inputs,
            *grads,
            specs=[VMEM] * len(inputs) + [ANY] * 2,
            out_specs=[ANY] * 2,
            scratch=[block, block, pltpu.SemaphoreType.DMA((2, own * len(which)))],
            aliases={1 + len(inputs) + i: i for i in range(2)},
        )
    grad_key, grad_value = grads
    return (grad_query, grad_key, grad_value, loss[0, 0])


def solution(mesh):
    return jax.shard_map(
        shards,
        mesh=mesh,
        in_specs=(
            P("seq", "head"),
            P("seq", "head"),
            P("seq", "head"),
            P("seq", "head"),
            P("head"),
            P("seq"),
        ),
        out_specs=(P("seq", "head"), P("seq", "head"), P("seq", "head"), P()),
        check_vma=False,
    )
```

```python
import functools

import jax
import jax.numpy as jnp
from jax import lax
from jax.experimental import pallas as pl
from jax.experimental.pallas import tpu as pltpu
from jax.sharding import PartitionSpec as P

HEAD_DIM = 128
TAIL = 8
epsilon = 1e-06
f32 = jnp.float32
bf16 = jnp.bfloat16
SMEM = pl.BlockSpec(memory_space=pltpu.SMEM)
VMEM = pl.BlockSpec(memory_space=pltpu.VMEM)
ANY = pl.BlockSpec(memory_space=pl.ANY)

NN = ((1,), (0,))
NT = ((1,), (1,))
TN = ((0,), (0,))


def split(x):
    high = x.astype(bf16)
    return high, (x - high.astype(f32)).astype(bf16)


def dot(a, b, dims):
    ca, cb = dims[0][0], dims[1][0]
    left = jnp.concatenate(a, axis=ca)
    both = jnp.concatenate(b, axis=1 - cb)
    right = jnp.concatenate([both, both], axis=cb)
    out = lax.dot_general(left, right, (dims, ((), ())), preferred_element_type=f32)
    n = out.shape[1] // 2
    return out[:, :n] + out[:, n:]


def head_cols(h):
    return pl.ds(pl.multiple_of(h * HEAD_DIM, HEAD_DIM), HEAD_DIM)


def rows_of(i):
    return slice(i * HEAD_DIM, (i + 1) * HEAD_DIM)


def in_hbm(x):
    return pltpu.with_memory_space_constraint(x, pltpu.HBM)


def shape(*s):
    return jax.ShapeDtypeStruct(s, f32)


def call(kernel, outs, flops, seat, *args, specs=None, out_specs=None, scratch=(), aliases=None, limit=24):
    specs = specs or [VMEM] * len(args)
    place = [] if seat is None else [seat]
    nbytes = sum(a.size * 4 for a in args) + sum(o.size * 4 for o in outs)
    return pl.pallas_call(
        kernel,
        out_shape=outs,
        in_specs=[SMEM] * len(place) + specs,
        out_specs=out_specs or [VMEM] * len(outs),
        scratch_shapes=scratch,
        input_output_aliases=aliases or {},
        compiler_params=pltpu.CompilerParams(vmem_limit_bytes=limit * 1024 * 1024),
        cost_estimate=pl.CostEstimate(flops=flops, bytes_accessed=nbytes, transcendentals=0),
    )(*place, *args)


def causal_mask(n):
    return lax.broadcasted_iota(jnp.int32, (n, n), 0) >= lax.broadcasted_iota(jnp.int32, (n, n), 1)


def column(row, n):
    return jnp.broadcast_to(row, (HEAD_DIM, n)).T


def pair_sum(parts):
    parts = list(parts)
    while len(parts) > 1:
        parts = [parts[i] + parts[i + 1] for i in range(0, len(parts), 2)]
    return parts[0]


class Plan:
    def __init__(self, length, heads, seq, head):
        group = 1
        while group < 4 and seq % (2 * group) == 0 and heads % (2 * group) == 0:
            group *= 2
        self.length, self.heads, self.head, self.group, self.own = length, heads, head, group, heads // group
        self.width, self.tokens = heads * HEAD_DIM * head, length * seq
        self.bits = [group << i for i in range(30) if group << i < seq]
        self.swaps = [bit | (bit // 2 if bit == group else 0) for bit in self.bits]
        self.state_rows = self.own * HEAD_DIM
        self.last = group // 2
        self.body = slice(0, self.state_rows)
        self.tail = slice(self.state_rows, self.state_rows + TAIL)

    def owned(self, seat, x):
        return (seat % self.group) ^ ((seat & self.group) // 2) ^ x

    def head_of(self, seat, x, i):
        return self.owned(seat, x) * self.own + i

    def share(self, seat, x, count=1):
        start = self.owned(seat, x) // count * (count * self.state_rows)
        return pl.ds(pl.multiple_of(start, HEAD_DIM), count * self.state_rows)


def outer_sum(plan, seat, reverse, totals):
    total = jnp.zeros((plan.state_rows, HEAD_DIM), f32)
    for bit, other in zip(plan.bits, totals):
        upper = (seat & bit) != 0
        counts = jnp.logical_not(upper) if reverse else upper
        total = total + jnp.where(counts, other[plan.body, :], 0.0)
    return total


def state_at(plan, seat, reverse, x, outer, parts):
    here = seat % plan.group
    total = outer
    for y in range(plan.group):
        if y != x:
            ahead = (here ^ y) > (here ^ x) if reverse else (here ^ y) < (here ^ x)
            total = total + jnp.where(ahead, parts[y][plan.body, :], 0.0)
    return total


def state_kernel(plan, k_hbm, v_hbm, *refs):
    group = plan.group
    out, (k, v, sems) = refs[:group], refs[group:]
    seat = lax.axis_index("seq")
    pair = min(group, 2)
    copies = {}
    for x in range(0, group, pair):
        cols = plan.share(seat, x, pair)
        copies[x] = [
            pltpu.make_async_copy(src.at[:, cols], dst.at[:, cols], sems.at[i, x])
            for i, (src, dst) in enumerate(((k_hbm, k), (v_hbm, v)))
        ]
        for copy in copies[x]:
            copy.start()
    for x in range(group):
        for copy in copies.get(x, ()):
            copy.wait()
        for i in range(plan.own):
            cols = head_cols(plan.head_of(seat, x, i))
            out[x][rows_of(i), :] = dot(split(k[:, cols]), split(v[:, cols]), TN)


def local_kernel(plan, seat, q_hbm, k, v, target_hbm, gain, mask, q, flipped, scores, local, aim, count, target, sems):
    copies = [
        pltpu.make_async_copy(src, dst, sems.at[i]) for i, (src, dst) in enumerate(((q_hbm, q), (target_hbm, target)))
    ]
    for copy in copies:
        copy.start()
    causal = causal_mask(plan.length)
    valid = mask[...].astype(f32)
    count[...] = jnp.full((TAIL, HEAD_DIM), jnp.sum(valid), f32)
    valid = column(valid, plan.length)
    for copy in copies:
        copy.wait()
    for h in range(plan.heads):
        cols = head_cols(h)
        flipped[h] = q[:, cols].T
        s = dot(split(q[:, cols]), split(k[:, cols]), NT)
        s = jnp.where(causal, s, 0.0)
        scores[h] = s
        local[:, cols] = dot(split(s), split(v[:, cols]), NN)
        aim[:, cols] = valid * (gain[:, cols] * target[:, cols])


def total_kernel(plan, seat, *refs):
    parts, out = refs[:-1], refs[-1]
    out[plan.body, :] = pair_sum(r[plan.body, :] for r in parts)
    if out.shape[0] > plan.state_rows:
        out[plan.tail, :] = parts[0][plan.tail, :] + parts[plan.last][plan.tail, :]


def prior_kernel(plan, seat, *refs):
    group = plan.group
    parts, totals, outs = refs[:group], refs[group : -group - 1], refs[-group:]
    outer = outer_sum(plan, seat[0], False, totals)
    for x in range(group):
        outs[x][...] = state_at(plan, seat[0], False, x, outer, parts)


def attend_kernel(plan, which, last, seat, q, local, aim, *refs):
    n = len(which)
    priors, refs = refs[:n], refs[n:]
    if last:
        squares, dots = refs[0][...], refs[1][...]
        refs = refs[2:]
    else:
        squares = jnp.zeros((plan.length, HEAD_DIM), f32)
        dots = jnp.zeros((plan.length, HEAD_DIM), f32)
    attended, sums = refs[:n], refs[n:]
    for x, prior, out in zip(which, priors, attended):
        for i in range(plan.own):
            cols = head_cols(plan.head_of(seat[0], x, i))
            a = local[:, cols] + dot(split(q[:, cols]), split(prior[rows_of(i), :]), NN)
            out[:, rows_of(i)] = a
            squares = squares + a * a
            dots = dots + aim[:, cols] * a
    if last:
        (stats,) = sums
        stats[0:1, :] = jnp.sum(squares.T, axis=0, keepdims=True)
        stats[1:2, :] = jnp.sum(dots.T, axis=0, keepdims=True)
        stats[2:, :] = jnp.zeros((TAIL - 2, plan.length), f32)
    else:
        sums[0][...] = squares
        sums[1][...] = dots


def scales(plan, stats):
    squares, dots = stats[0:1, :], stats[1:2, :]
    inverse_rms = lax.rsqrt(squares / plan.width + epsilon)
    loss = inverse_rms * dots
    return inverse_rms, inverse_rms * inverse_rms * loss / plan.width, loss


def grad_kernel(plan, seat, flipped, aim, count, *refs):
    refs = list(refs)
    take = lambda n: [refs.pop(0) for _ in range(n)]
    attended, stat_parts, (factors,), out = take(plan.group), take(plan.head), take(1), take(plan.group)
    left, right, losses = scales(plan, pair_sum(r[...] for r in stat_parts))
    factors[0:1, :] = left
    factors[1:2, :] = right
    left, right = column(left, plan.length), column(right, plan.length)
    row = lax.broadcasted_iota(jnp.int32, (TAIL, HEAD_DIM), 0)
    tail = jnp.where(row == 0, jnp.sum(losses), count[...])
    for x in range(plan.group):
        for i in range(plan.own):
            h = plan.head_of(seat[0], x, i)
            cols = head_cols(h)
            g = left * aim[:, cols] - right * attended[x][:, rows_of(i)]
            out[x][rows_of(i), :] = dot(split(flipped[h]), split(g), NN)
        if x in (0, plan.last):
            out[x][plan.tail, :] = tail


def local_grad_kernel(plan, seat, q, k, v, aim, factors, scores, *refs):
    group = plan.group
    attended, priors, (grad_q, grad_k, grad_v) = refs[:group], refs[group : 2 * group], refs[2 * group :]
    left, right = column(factors[0:1, :], plan.length), column(factors[1:2, :], plan.length)
    causal = causal_mask(plan.length)
    for x in range(plan.group):
        for i in range(plan.own):
            h = plan.head_of(seat[0], x, i)
            cols = head_cols(h)
            g = split(left * aim[:, cols] - right * attended[x][:, rows_of(i)])
            gs = split(jnp.where(causal, dot(g, split(v[:, cols]), NT), 0.0))
            prior = split(priors[x][rows_of(i), :])
            grad_q[:, cols] = dot(gs, split(k[:, cols]), NN) + dot(g, prior, NT)
            grad_k[:, cols] = dot(gs, split(q[:, cols]), TN)
            grad_v[:, cols] = dot(split(scores[h]), g, TN)


def later_kernel(plan, seat, *refs):
    group = plan.group
    states, totals, outs = refs[:group], refs[group : -group - 1], refs[-group:]
    outer = outer_sum(plan, seat[0], True, totals[1:])
    tail = totals[0][plan.tail, :]
    for other in totals[1:]:
        tail = tail + other[plan.tail, :]
    for x in range(group):
        outs[x][plan.body, :] = state_at(plan, seat[0], True, x, outer, states)
        if x == min(1, group - 1):
            outs[x][plan.tail, :] = tail


def final_kernel(plan, which, seat, k, v, part_k, part_v, sent, *refs):
    n = len(which)
    first = which[0] == 0
    later, refs = list(refs[:n]), refs[n:]
    if first:
        (part_q, loss, grad_q, grad_k, grad_v, block_k, block_v, block_q, sems) = refs
        tail = later[-1][plan.tail, :]
    else:
        (tail_ref, _, _, grad_k, grad_v, block_k, block_v, sems) = refs
        tail = tail_ref[plan.tail, :]
    if plan.group > 1:
        tail = sent[plan.tail, :] + tail
    factor = plan.tokens / tail[1:2, 0:1]
    copies = []
    for j, x in enumerate(which):
        for i in range(plan.own):
            cols = head_cols(plan.head_of(seat[0], x, i))
            state = split(later[j][rows_of(i), :])
            block_k[j, :, rows_of(i)] = factor * (part_k[:, cols] + dot(split(v[:, cols]), state, NT))
            block_v[j, :, rows_of(i)] = factor * (part_v[:, cols] + dot(split(k[:, cols]), state, NN))
            for m, (block, out) in enumerate(((block_k, grad_k), (block_v, grad_v))):
                copies.append(
                    pltpu.make_async_copy(block.at[j, :, rows_of(i)], out.at[:, cols], sems.at[m, j * plan.own + i])
                )
                copies[-1].start()
    if first:
        block_q[...] = factor * part_q[...]
        copies.append(pltpu.make_async_copy(block_q, grad_q, sems.at[2, 0]))
        copies[-1].start()
        loss[...] = tail[0:1, 0:1] / tail[1:2, 0:1]
    for copy in copies:
        copy.wait()


def swap(value, axis, step):
    return lax.ppermute(value, axis, [(i, i ^ step) for i in range(lax.axis_size(axis))])


def swap_all(parts, axis):
    return [parts[0]] + [swap(part, axis, x) for x, part in enumerate(parts) if x]


def swap_totals(plan, total):
    totals = [total]
    for step in plan.swaps:
        totals.append(swap(total, "seq", step))
        if step != plan.swaps[-1]:
            total = total + totals[-1]
    return totals


def shards(queries, key_rows, value_rows, target, norm_gain, valid_mask):
    length, columns = queries.shape
    heads = columns // HEAD_DIM
    head_count = lax.axis_size("head")
    plan = Plan(length, heads, lax.axis_size("seq"), head_count)
    group, own = plan.group, plan.own
    product = 6 * HEAD_DIM**3 * heads
    seat = jnp.reshape(lax.axis_index("seq"), (1,)).astype(jnp.int32)
    gain = norm_gain.reshape(1, columns)
    mask = valid_mask.reshape(1, length)
    sum_shape = shape(plan.state_rows + TAIL, HEAD_DIM)
    state = shape(plan.state_rows, HEAD_DIM)
    piece = shape(length, plan.state_rows)
    wide = shape(length, columns)
    bind = lambda kernel: functools.partial(kernel, plan)

    *kv, key_rows, value_rows = call(
        bind(state_kernel),
        [state] * group + [wide] * 2,
        product,
        None,
        in_hbm(key_rows),
        in_hbm(value_rows),
        specs=[ANY] * 2,
        scratch=[pltpu.SemaphoreType.DMA((2, group))],
    )
    queries, flipped, scores, local, aim, count = call(
        bind(local_kernel),
        [wide, shape(heads, HEAD_DIM, length), shape(heads, length, length), wide, wide, shape(TAIL, HEAD_DIM)],
        2 * product,
        seat,
        in_hbm(queries),
        key_rows,
        value_rows,
        in_hbm(target),
        in_hbm(gain),
        in_hbm(mask),
        specs=[ANY, VMEM, VMEM, ANY, VMEM, VMEM],
        scratch=[pltpu.VMEM((length, columns), f32), pltpu.SemaphoreType.DMA((2,))],
    )
    kv = swap_all(kv, "seq")
    (total,) = call(bind(total_kernel), [state], 0, seat, *kv)
    totals = swap_totals(plan, total)
    priors = call(
        bind(prior_kernel),
        [state] * group,
        0,
        seat,
        *kv,
        *totals[1:],
        scores,
        specs=[VMEM] * (group + len(totals) - 1) + [ANY],
    )
    priors = swap_all(priors, "seq")
    early, late = list(range(group - 1)), [group - 1]
    column_sum = shape(length, HEAD_DIM)
    *attended, squares, dots = call(
        functools.partial(attend_kernel, plan, early, False),
        [piece] * len(early) + [column_sum] * 2,
        product,
        seat,
        queries,
        local,
        aim,
        *priors[:-1],
    )
    last, stats = call(
        functools.partial(attend_kernel, plan, late, True),
        [piece, shape(TAIL, length)],
        product // group,
        seat,
        queries,
        local,
        aim,
        priors[-1],
        squares,
        dots,
    )
    attended.append(last)
    stats = swap_all([stats] * head_count, "head")
    factors, *states = call(
        bind(grad_kernel),
        [shape(TAIL, length)] + [sum_shape if x in (0, plan.last) else state for x in range(group)],
        product,
        seat,
        flipped,
        aim,
        count,
        *attended,
        *stats,
    )
    part_query, part_key, part_value = call(
        bind(local_grad_kernel), [wide] * 3, 5 * product, seat, queries, key_rows, value_rows, aim, factors, scores, *attended, *priors
    )
    states = swap_all(states, "seq")
    (grad_total,) = call(bind(total_kernel), [sum_shape], 0, seat, *states)
    grad_totals = swap_totals(plan, grad_total)
    later = call(
        bind(later_kernel),
        [sum_shape if x == min(1, group - 1) else state for x in range(group)],
        0,
        seat,
        *states,
        *grad_totals,
        part_key,
        specs=[VMEM] * (group + len(grad_totals)) + [ANY],
    )
    sent = later[min(1, group - 1)]
    later = swap_all(later, "seq")
    grads = []
    for which in [early[:2], early[2:] + late]:
        block = pltpu.VMEM((len(which), length, plan.state_rows), f32)
        inputs = [key_rows, value_rows, part_key, part_value, sent, *(later[x] for x in which)]
        if not grads:
            loss, grad_query, *grads = call(
                functools.partial(final_kernel, plan, which),
                [shape(1, 1), wide, wide, wide],
                2 * product * len(which) // group,
                seat,
                *inputs,
                part_query,
                out_specs=[VMEM] + [ANY] * 3,
                scratch=[block, block, pltpu.VMEM((length, columns), f32), pltpu.SemaphoreType.DMA((3, own * len(which)))],
            )
            continue
        inputs.append(later[1])
        grads = call(
            functools.partial(final_kernel, plan, which),
            [wide] * 2,
            2 * product * len(which) // group,
            seat,
            *inputs,
            *grads,
            specs=[VMEM] * len(inputs) + [ANY] * 2,
            out_specs=[ANY] * 2,
            scratch=[block, block, pltpu.SemaphoreType.DMA((2, own * len(which)))],
            aliases={1 + len(inputs) + i: i for i in range(2)},
        )
    grad_key, grad_value = grads
    return (grad_query, grad_key, grad_value, loss[0, 0])


def solution(mesh):
    return jax.shard_map(
        shards,
        mesh=mesh,
        in_specs=(
            P("seq", "head"),
            P("seq", "head"),
            P("seq", "head"),
            P("seq", "head"),
            P("head"),
            P("seq"),
        ),
        out_specs=(P("seq", "head"), P("seq", "head"), P("seq", "head"), P()),
        check_vma=False,
    )
```
